512 devices in a mesh: dp: 32 (over x, z), hid: 16 (over y, core).
Axes of the slice: x: 4, y: 8, z: 8, core: 2. Of those that a mesh axis runs over, the one named last changes fastest.
Arguments:
- inputs: bfloat16 [8192, 8192], P('dp', 'hid'), may hold values from -6 to 6
- out_grad: bfloat16 [8192, 8192], P('dp', 'hid'), may hold values from -6 to 6
- home_block: int32 [64], P('hid'), may hold values from 0 to 1
- blocks_up: bfloat16 [64, 3, 256, 256], P('hid', None, 'dp'), may hold values from -0.21875 to 0.21875
- blocks_down: bfloat16 [64, 3, 256, 256], P('hid', None, 'dp'), may hold values from -0.15625 to 0.15625
- up_left: bfloat16 [8192, 128], P('hid', 'dp'), may hold values from -0.0625 to 0.0625
- up_right: bfloat16 [128, 16384], P('dp', 'hid'), may hold values from -0.5 to 0.5
- down_left: bfloat16 [16384, 128], P('hid', 'dp'), may hold values from -0.046875 to 0.046875
- down_right: bfloat16 [128, 8192], P('dp', 'hid'), may hold values from -0.5 to 0.5
Outputs:
- outputs: bfloat16 [8192, 8192], P('dp', 'hid')
- input_grad: bfloat16 [8192, 8192], P('dp', 'hid')
- grad_blocks_up: bfloat16 [64, 3, 256, 256], P('hid', None, 'dp')
- grad_blocks_down: bfloat16 [64, 3, 256, 256], P('hid', None, 'dp')
- grad_up_left: bfloat16 [8192, 128], P('hid', 'dp')
- grad_up_right: bfloat16 [128, 16384], P('dp', 'hid')
- grad_down_left: bfloat16 [16384, 128], P('hid', 'dp')
- grad_down_right: bfloat16 [128, 8192], P('dp', 'hid')
The draws below stay inside these ranges and needn't reach their ends.
All inputs are finite; a program needn't handle non-finite values.
Results may differ from the reference program's by a relative error of at most 0.022.
Values may be sent and summed in bfloat16 or wider, within the bound.
A program may use at most 64 MiB of HBM per device.

```python
import jax
import jax.numpy as jnp
from jax import lax

D = 8192
H = 16384
BLK = 256
R = 128
LEVELS = 2
TOK_DEV = 256
TOKENS = 8192
NDB = 32
NHB = 64
IB_DEV = 2
HB_DEV = 4
N_DP = 32
N_HID = 16


def plant(values, rng, smallest, high):
    place = [jax.random.randint(jax.random.fold_in(rng, axis), (), 0, length) for axis, length in enumerate(values.shape)]
    widest = values.shape.index(max(values.shape))
    next_to = place[:widest] + [(place[widest] + 1) % values.shape[widest]] + place[widest + 1:]
    return values.at[tuple(place)].set(smallest).at[tuple(next_to)].set(high)


def block_levels(rng, extent, shards, low, largest):
    loudness = 1.0
    for axis_at, parts in shards:
        draws = jax.random.uniform(jax.random.fold_in(jax.random.fold_in(rng, 6), axis_at), (parts,), jnp.float32, low / len(shards), largest / len(shards))
        loudness = loudness * jnp.repeat(jnp.exp(draws), extent[axis_at] // parts).reshape((-1,) + (1,) * (len(extent) - 1 - axis_at))
    return loudness


def gaussian(key, dims, deviation, reach, pieces=(), kind=jnp.bfloat16):
    level = block_levels(key, dims, pieces, -0.22, 0.18) if pieces else 1.0
    values = jax.random.normal(key, dims, jnp.float32) * deviation * level
    return jnp.minimum(jnp.maximum(values, -reach), reach).astype(kind)


def setup_inputs(seed: int = 0) -> dict:
    streams_of = jax.random.split(jax.random.key(seed), 10)
    return {
        "inputs": gaussian(streams_of[0], (TOKENS, D), 1.0, 6.0, ((0, 32), (1, 16))),
        "out_grad": gaussian(streams_of[1], (TOKENS, D), 1.0, 6.0, ((0, 32), (1, 16))),
        "home_block": plant(jax.random.randint(streams_of[2], (NHB,), 0, IB_DEV), jax.random.fold_in(streams_of[2], 1), 0, IB_DEV - 1).astype(jnp.int32),
        "blocks_up": gaussian(streams_of[3], (NHB, LEVELS + 1, BLK, BLK), ((LEVELS + 1) * BLK) ** -0.5, 0.21875, ((0, 16), (2, 32))),
        "blocks_down": gaussian(streams_of[4], (NHB, LEVELS + 1, BLK, BLK), ((LEVELS + 1) * H // D * BLK) ** -0.5, 0.15625, ((0, 16), (2, 32))),
        "up_left": gaussian(streams_of[5], (D, R), D ** -0.5, 0.0625, ((0, 16), (1, 32))),
        "up_right": gaussian(streams_of[6], (R, H), R ** -0.5, 0.5, ((0, 32), (1, 16))),
        "down_left": gaussian(streams_of[7], (H, R), H ** -0.5, 0.046875, ((0, 16), (1, 32))),
        "down_right": gaussian(streams_of[8], (R, D), R ** -0.5, 0.5, ((0, 32), (1, 16))),
    }


gelu_coef = 0.7978845608028654
cubic_coef = 0.044715


def gelu_pair(pre_act):
    tangent = jnp.tanh(gelu_coef * (pre_act + cubic_coef * pre_act * pre_act * pre_act))
    activated = 0.5 * pre_act * (1.0 + tangent)
    derivative = 0.5 * (1.0 + tangent) + 0.5 * pre_act * (1.0 - tangent * tangent) * gelu_coef * (1.0 + 3.0 * cubic_coef * pre_act * pre_act)
    return activated, derivative


def make_table(home_block):
    hidden_ids = jnp.arange(NHB, dtype=jnp.int32)
    owner_dev = hidden_ids // HB_DEV
    columns = [owner_dev]
    for level_idx in range(LEVELS):
        columns.append(jnp.bitwise_xor(owner_dev, N_HID // (2 ** (level_idx + 1))))
    devices = jnp.stack(columns, axis=1)
    return (devices * IB_DEV + home_block[:, None]).astype(jnp.int32)


def rounded(array):
    return lax.optimization_barrier(array.astype(jnp.bfloat16)).astype(jnp.float32)


def reference(inputs, out_grad, home_block, blocks_up, blocks_down, up_left, up_right, down_left, down_right):
    single = jnp.float32
    highest = lax.Precision.HIGHEST
    block_table = make_table(home_block)
    one_hot = (block_table[:, :, None] == jnp.arange(NDB, dtype=jnp.int32)[None, None, :]).astype(single)
    up_full = blocks_up.astype(single)
    down_full = blocks_down.astype(single)
    grad_scale = float(TOKENS) ** -0.5

    def group_pass(carry_sums, group_rows):
        rows_in, rows_grad = group_rows
        row_count = rows_in.shape[0]
        picked = rows_in.astype(single).reshape(row_count, NDB, BLK)[:, block_table, :]
        rank_in = jnp.dot(rows_in, up_left, preferred_element_type=single).astype(jnp.bfloat16)
        pre_act = jnp.einsum("thsk,hskn->thn", picked, up_full).reshape(row_count, H)
        pre_act = pre_act + jnp.dot(rank_in, up_right, preferred_element_type=single)
        activated, derivative = gelu_pair(pre_act)
        hidden = activated.astype(jnp.bfloat16)
        hidden_full = hidden.astype(single).reshape(row_count, NHB, BLK)
        rank_mid = jnp.dot(hidden, down_left, preferred_element_type=single).astype(jnp.bfloat16)
        terms = jnp.einsum("thk,hskn->tshn", hidden_full, down_full)
        placed = jnp.einsum("tshn,hsj->tsjn", terms, one_hot, precision=highest)
        total = placed[:, 0]
        for level_idx in range(LEVELS):
            total = total + placed[:, level_idx + 1]
        outputs = (total.reshape(row_count, D) + jnp.dot(rank_mid, down_right, preferred_element_type=single)).astype(jnp.bfloat16)
        rank_back = jnp.dot(rows_grad, down_right.T, preferred_element_type=single).astype(jnp.bfloat16)
        grad_picked = rows_grad.astype(single).reshape(row_count, NDB, BLK)[:, block_table, :]
        grad_hidden = jnp.einsum("thsn,hskn->thk", grad_picked, down_full).reshape(row_count, H)
        grad_hidden = grad_hidden + jnp.dot(rank_back, down_left.T, preferred_element_type=single)
        grad_pre = (grad_hidden * derivative).astype(jnp.bfloat16)
        grad_full = grad_pre.astype(single).reshape(row_count, NHB, BLK)
        rank_grad = jnp.dot(grad_pre, up_right.T, preferred_element_type=single).astype(jnp.bfloat16)
        back_terms = jnp.einsum("thn,hskn->tshk", grad_full, up_full)
        back_placed = jnp.einsum("tshk,hsj->tsjk", back_terms, one_hot, precision=highest)
        back_total = back_placed[:, 0]
        for level_idx in range(LEVELS):
            back_total = back_total + back_placed[:, level_idx + 1]
        input_grad = (back_total.reshape(row_count, D) + jnp.dot(rank_grad, up_left.T, preferred_element_type=single)).astype(jnp.bfloat16)
        group_terms = (
            jnp.einsum("thsk,thn->hskn", picked, grad_full),
            jnp.einsum("thk,thsn->hskn", hidden_full, grad_picked),
            jnp.dot(rows_in.T, rank_grad, preferred_element_type=single),
            jnp.dot(rank_in.T, grad_pre, preferred_element_type=single),
            jnp.dot(hidden.T, rank_back, preferred_element_type=single),
            jnp.dot(rank_mid.T, rows_grad, preferred_element_type=single),
        )
        new_sums = tuple(running + rounded(grad_scale * term_now) for running, term_now in zip(carry_sums, group_terms))
        return new_sums, (outputs, input_grad)

    initial = tuple(jnp.zeros(shape_now, single) for shape_now in (blocks_up.shape, blocks_down.shape, up_left.shape, up_right.shape, down_left.shape, down_right.shape))
    groups = (inputs.reshape(N_DP, TOK_DEV, D), out_grad.reshape(N_DP, TOK_DEV, D))
    sums_all, (outs_all, grads_all) = lax.scan(group_pass, initial, groups)
    return (outs_all.reshape(TOKENS, D), grads_all.reshape(TOKENS, D),
            sums_all[0].astype(jnp.bfloat16), sums_all[1].astype(jnp.bfloat16),
            sums_all[2].astype(jnp.bfloat16), sums_all[3].astype(jnp.bfloat16),
            sums_all[4].astype(jnp.bfloat16), sums_all[5].astype(jnp.bfloat16))
```

```python
import functools

import jax
import jax.numpy as jnp
from jax import lax
from jax.experimental import pallas as pl
from jax.experimental.pallas import tpu as pltpu
from jax.sharding import PartitionSpec as P

MESH = pl.DeviceIdType.MESH
gelu_coef = 0.7978845608028654
cubic_coef = 0.044715
SLOTS = 3
F32 = jnp.float32
BF16 = jnp.bfloat16
NN = (((1,), (0,)), ((), ()))
NT = (((1,), (1,)), ((), ()))


def dot(a, b, dims=NN):
    return lax.dot_general(a, b, dims, preferred_element_type=F32)


def flip(index, bit):
    return index + bit - 2 * bit * lax.rem(lax.div(index, bit), 2)


def wrap(value, n):
    return lax.rem(value + 4 * n, n)


def gelu_pair(pre_act):
    tangent = jnp.tanh(gelu_coef * (pre_act + cubic_coef * pre_act * pre_act * pre_act))
    activated = 0.5 * pre_act * (1.0 + tangent)
    derivative = 0.5 * (1.0 + tangent) + 0.5 * pre_act * (1.0 - tangent * tangent) * gelu_coef * (
        1.0 + 3.0 * cubic_coef * pre_act * pre_act
    )
    return activated, derivative


class Place:
    def __init__(self, nx, nz, nh):
        self.size = {"x": nx, "z": nz}
        self.nh = nh
        self.dp = lax.axis_index("dp")
        self.hid = lax.axis_index("hid")
        self.pos = {"x": lax.div(self.dp, nz), "z": lax.rem(self.dp, nz)}
        self.near = (self.dp, flip(self.hid, nh // 4))
        self.far = (self.dp, flip(flip(self.hid, nh // 4), nh // 2))

    def neighbour(self, axis, o):
        x, z = self.pos["x"], self.pos["z"]
        if axis == "x":
            x = wrap(x + o, self.size["x"])
        else:
            z = wrap(z + o, self.size["z"])
        return (x * self.size["z"] + z, self.hid)

    def peer(self, j):
        return (self.dp, lax.rem(self.hid + j, self.nh))


def gather_axes(kind):
    return ("x", "z") if kind < 2 else ("z", "x")


def ring_dirs(n):
    return [(0, n // 2)] + ([(1, n // 2 - 1)] if n > 2 else [])


class Gather:
    def __init__(self, place, buf, kind, width, send_sem, recv_sem):
        self.place, self.buf, self.kind = place, buf, kind
        self.columns = pl.ds(kind * width, width)
        self.send_sem, self.recv_sem = send_sem, recv_sem
        self.axes = gather_axes(kind)
        self.turns = [place.size[a] // 2 for a in self.axes]
        self.rounds = sum(self.turns)
        self.sent = {}

    def part(self, phase, at):
        axis = self.axes[phase]
        own = self.place.pos
        if phase == 0:
            x, z = (at, own["z"]) if axis == "x" else (own["x"], at)
            return self.buf.at[x, z, :, self.columns]
        if axis == "x":
            return self.buf.at[at, :, :, self.columns]
        return self.buf.at[:, at, :, self.columns]

    def copy(self, phase, d, t, at):
        axis = self.axes[phase]
        o = (1 if self.kind % 2 == 0 else -1) * (1 if d == 0 else -1)
        n = self.place.size[axis]
        first = 0 if phase == 0 else self.place.size[self.axes[0]] - 1
        slot = first + (n // 2 if d else 0) + t - 1
        ref = self.part(phase, wrap(self.place.pos[axis] - o * at, n))
        return pltpu.make_async_remote_copy(
            src_ref=ref,
            dst_ref=ref,
            send_sem=self.send_sem.at[self.kind, phase * 2 + d],
            recv_sem=self.recv_sem.at[self.kind, slot],
            device_id=self.place.neighbour(axis, o),
            device_id_type=MESH,
        )

    def send(self, phase, d, t):
        before = self.sent.pop((phase, d), None)
        if before is not None:
            before.wait_send()
        made = self.copy(phase, d, t, t - 1)
        made.start()
        self.sent[(phase, d)] = made

    def begin(self, phase):
        for d, count in ring_dirs(self.place.size[self.axes[phase]]):
            self.send(phase, d, 1)

    def advance(self, k):
        if k == 0:
            self.begin(0)
            return
        phase = 0 if k <= self.turns[0] else 1
        t = k - (self.turns[0] if phase else 0)
        for d, count in ring_dirs(self.place.size[self.axes[phase]]):
            if t <= count:
                self.copy(phase, d, t, t).wait_recv()
                if t < count:
                    self.send(phase, d, t + 1)
        if phase == 0 and t == self.turns[0]:
            self.begin(1)

    def finish(self):
        for made in self.sent.values():
            made.wait_send()
        self.sent = {}


class Scatter:
    def __init__(self, place, terms, kind, width, first_buf, second_buf, send_sem, recv_sem):
        self.place, self.terms, self.kind = place, terms, kind
        self.columns = pl.ds(kind * width, width)
        self.bufs = (first_buf, second_buf)
        self.send_sem, self.recv_sem = send_sem, recv_sem
        self.axes = gather_axes(kind)[::-1]
        self.turns = [place.size[a] // 2 for a in self.axes]
        self.rounds = sum(self.turns)
        self.sent = {}

    def term(self, phase, at):
        axis = self.axes[phase]
        own = self.place.pos
        if phase == 1:
            x, z = (at, own["z"]) if axis == "x" else (own["x"], at)
            return self.terms.at[x, z, :, self.columns]
        if axis == "x":
            return self.terms.at[at, :, :, self.columns]
        return self.terms.at[:, at, :, self.columns]

    def slot(self, phase, d, t):
        n = self.place.size[self.axes[phase]]
        return (n // 2 if d else 0) + t - 1

    def arrived(self, phase, d, t):
        return self.bufs[phase].at[self.kind % 2, self.slot(phase, d, t)]

    def o(self, d):
        return (1 if self.kind % 2 == 0 else -1) * (1 if d == 0 else -1)

    def copy(self, phase, d, t, source):
        axis = self.axes[phase]
        first = 0 if phase == 0 else self.place.size[self.axes[0]] - 1
        return pltpu.make_async_remote_copy(
            src_ref=source,
            dst_ref=self.arrived(phase, d, t),
            send_sem=self.send_sem.at[self.kind, phase * 2 + d],
            recv_sem=self.recv_sem.at[self.kind, first + self.slot(phase, d, t)],
            device_id=self.place.neighbour(axis, self.o(d)),
            device_id_type=MESH,
        )

    def send(self, phase, d, t, source):
        before = self.sent.pop((phase, d), None)
        if before is not None:
            before.wait_send()
        made = self.copy(phase, d, t, source)
        made.start()
        self.sent[(phase, d)] = made

    def dest(self, phase, d, t, count):
        axis = self.axes[phase]
        return wrap(self.place.pos[axis] + self.o(d) * (count - t + 1), self.place.size[axis])

    def begin(self, phase):
        for d, count in ring_dirs(self.place.size[self.axes[phase]]):
            self.send(phase, d, 1, self.term(phase, self.dest(phase, d, 1, count)))

    def advance(self, k):
        if k == 0:
            self.begin(0)
            return
        phase = 0 if k <= self.turns[0] else 1
        t = k - (self.turns[0] if phase else 0)
        axis = self.axes[phase]
        dirs = ring_dirs(self.place.size[axis])
        for d, count in dirs:
            if t <= count:
                held = self.arrived(phase, d, t)
                self.copy(phase, d, t, held).wait_recv()
                if t < count:
                    held[...] = held[...] + self.term(phase, self.dest(phase, d, t + 1, count))[...]
                    self.send(phase, d, t + 1, held)
        if t == self.turns[phase]:
            own = self.term(phase, self.place.pos[axis])
            total = own[...].astype(F32)
            for d, count in dirs:
                total = total + self.arrived(phase, d, count)[...].astype(F32)
            if phase == 0:
                own[...] = total.astype(BF16)
                self.begin(1)
            else:
                self.result = total

    def finish(self):
        for made in self.sent.values():
            made.wait_send()
        self.sent = {}


class RankSum:
    def __init__(self, place, parts, arrived, whole, sems):
        self.place, self.parts, self.got, self.whole, self.sems = place, parts, arrived, whole, sems

    def scatter_copy(self, j):
        peer = self.place.peer(j)
        return pltpu.make_async_remote_copy(
            src_ref=self.parts.at[peer[1]],
            dst_ref=self.got.at[j],
            send_sem=self.sems.at[0, j],
            recv_sem=self.sems.at[1, j],
            device_id=peer,
            device_id_type=MESH,
        )

    def gather_copy(self, j, at):
        return pltpu.make_async_remote_copy(
            src_ref=self.whole.at[at],
            dst_ref=self.whole.at[at],
            send_sem=self.sems.at[2, j],
            recv_sem=self.sems.at[3, j],
            device_id=self.place.peer(j),
            device_id_type=MESH,
        )

    def each(self, body):
        @pl.loop(1, self.place.nh)
        def _(j):
            body(j)

    def start(self):
        self.each(lambda j: self.scatter_copy(j).start())

    def middle(self):
        self.each(lambda j: self.scatter_copy(j).wait_recv())
        me = self.place.hid
        total = self.parts[me].astype(F32)
        for j in range(1, self.place.nh):
            total = total + self.got[j].astype(F32)
        self.whole[me] = total.astype(BF16)
        self.each(lambda j: self.gather_copy(j, me).start())

    def end(self):
        nh = self.place.nh

        def wait(j):
            self.gather_copy(j, lax.rem(self.place.hid + nh - j, nh)).wait_recv()

        self.each(wait)

    def finish(self):
        def wait(j):
            self.scatter_copy(j).wait_send()
            self.gather_copy(j, self.place.hid).wait_send()

        self.each(wait)


def layer(
    nx, nz, nh, scale,
    x_ref, g_ref, home, bu_ref, bd_ref, ul_ref, ur_ref, dl_ref, dr_ref,
    out_ref, ig_ref, gbu_ref, gbd_ref, gul_ref, gur_ref, gdl_ref, gdr_ref,
    g_low, g_up, g_down, t_low, t_up, t_down,
    low_z1, low_x2, low_x1, low_z2, up_z1, up_x2, up_x1, up_z2, dn_z1, dn_x2, dn_x1, dn_z2,
    w_up, w_down, m_low, xs, gs, xt, pre, der, hid_t, gp, hid_m, gp_m,
    rank_parts, rank_got, rank_one, rank_two,
    side_send, side_mid, side_end,
    ag_send, ag_recv, rs_send, rs_recv, rank_sems, y_sems,
):
    place = Place(nx, nz, nh)
    rows, blk = bu_ref.shape[2], bu_ref.shape[3]
    tokens = x_ref.shape[0]
    hb = bu_ref.shape[0]
    half = rows // 2
    px, pz = place.pos["x"], place.pos["z"]

    barrier = pltpu.get_barrier_semaphore()
    for axis in ("x", "z"):
        for o in (1, -1):
            pl.semaphore_signal(barrier, inc=1, device_id=place.neighbour(axis, o), device_id_type=MESH)

    @pl.loop(1, nh)
    def _(j):
        pl.semaphore_signal(barrier, inc=1, device_id=place.peer(j), device_id_type=MESH)

    hidden_dev, width_dev = ur_ref.shape[1], dr_ref.shape[1]
    g_low[px, pz, :, 0:hidden_dev] = jnp.concatenate(
        [ur_ref[...].astype(F32), dl_ref[...].astype(F32)], axis=0
    ).astype(BF16)
    g_low[px, pz, :, hidden_dev:] = jnp.concatenate(
        [ul_ref[...].astype(F32), dr_ref[...].astype(F32)], axis=0
    ).astype(BF16)
    for s in range(SLOTS):
        for h in range(hb):
            at = (s * hb + h) * blk
            g_up[px, pz, :, at : at + blk] = bu_ref[h, s]
            g_down[px, pz, :, at : at + blk] = bd_ref[h, s]
    for b in range(2):
        xs[0, b] = x_ref[:, b * blk : (b + 1) * blk]
        gs[0, b] = g_ref[:, b * blk : (b + 1) * blk]
    pl.semaphore_wait(barrier, 4 + nh - 1)

    groups = (g_low, g_up, g_down)
    gathers = [
        [
            Gather(place, buf, kind, buf.shape[3] // 4, ag_send.at[i], ag_recv.at[i])
            for kind in range(4)
        ]
        for i, buf in enumerate(groups)
    ]
    rounds = nx // 2 + nz // 2

    def gather_step(i, k):
        for one in gathers[i]:
            one.advance(k)

    part = tokens // 2
    pieces = [(ref, b, q) for ref in (xs, gs) for b in range(2) for q in range(2)]

    def y_copy(i, stage):
        ref, b, q = pieces[i]
        at = pl.ds(q * part, part)
        return pltpu.make_async_remote_copy(
            src_ref=ref.at[0 if stage == 0 else 2, b, at],
            dst_ref=ref.at[2 if stage == 0 else 1, b, at],
            send_sem=y_sems.at[stage, 0, i],
            recv_sem=y_sems.at[stage, 1, i],
            device_id=place.near if stage == 0 else place.far,
            device_id_type=MESH,
        )

    gather_step(0, 0)
    for i in range(4):
        y_copy(i, 0).start()
    gather_step(1, 0)
    for i in range(4, 8):
        y_copy(i, 0).start()
    gather_step(2, 0)

    def pass_on(i):
        y_copy(i, 0).wait_recv()
        y_copy(i, 1).start()

    column = lax.broadcasted_iota(jnp.int32, (tokens, blk), 1)
    is_low = lax.rem(column, rows) < half

    def flat(buf, at, width):
        return buf[:, :, :, at : at + width].astype(F32).reshape(blk, width).astype(BF16)

    one = RankSum(place, rank_parts.at[0], rank_got.at[0], rank_one, rank_sems.at[0])
    two = RankSum(place, rank_parts.at[1], rank_got.at[1], rank_two, rank_sems.at[1])

    def rank_start(which, index, low, high):
        mixed = jnp.where(is_low, low, high).reshape(nh, tokens // nh, blk)
        rank_parts[index] = mixed.astype(BF16)
        which.start()

    passed = 0
    for k in range(1, rounds + 3):
        for i in range(3):
            if 1 <= k - i <= rounds:
                gather_step(i, k - i)
        if k == rounds:
            for j in range(6):
                m_low[:, j * blk : (j + 1) * blk] = flat(g_low, j * blk, blk)
            rank_start(
                one,
                0,
                dot(x_ref[...], m_low[:, hidden_dev:], NT),
                dot(g_ref[...], m_low[:, hidden_dev:], NT),
            )
        while passed < min(8, k):
            pass_on(passed)
            passed += 1
        if k == rounds + 1:
            for j in range(SLOTS * hb):
                w_up[j // hb, :, (j % hb) * blk : (j % hb + 1) * blk] = flat(g_up, j * blk, blk)
    while passed < 8:
        pass_on(passed)
        passed += 1
    one.middle()
    for j in range(SLOTS * hb):
        w_down[j // hb, (j % hb) * blk : (j % hb + 1) * blk, :] = flat(g_down, j * blk, blk)
    for i in range(8):
        y_copy(i, 1).wait_recv()
    for s in range(SLOTS):
        for b in range(2):
            xt[s, b] = xs[s, b].T

    one.end()
    rank1 = rank_one[...].reshape(tokens, blk)
    zero = jnp.zeros_like(rank1)
    rank_in = jnp.where(is_low, rank1, zero)
    rank_back = jnp.where(is_low, zero, rank1)

    @pl.loop(0, hb)
    def _(h):
        home_h = home[h]
        at = pl.ds(pl.multiple_of(h * blk, blk), blk)
        value = dot(rank_in, m_low[:, at])
        grad = dot(rank_back, m_low[:, at])
        for s in range(SLOTS):
            value = value + dot(xs[s, home_h], w_up[s, :, at])
            grad = grad + dot(gs[s, home_h], w_down[s, at, :], NT)
        activated, derivative = gelu_pair(value)
        hidden = activated.astype(BF16)
        grad_pre = (grad * derivative).astype(BF16)
        hid_t[h] = hidden.T
        gp[h] = grad_pre
        for b in range(2):
            keep = jnp.where(home_h == b, 1.0, 0.0).astype(F32)
            hid_m[b, :, at] = (hidden.astype(F32) * keep).astype(BF16)
            gp_m[b, :, at] = (grad_pre.astype(F32) * keep).astype(BF16)

    def side(tensor, s, b):
        if tensor == 0:
            return dot(hid_m[b], w_down[s])
        return dot(gp_m[b], w_up[s], NT)

    sides = [(tensor, b) for tensor in range(2) for b in range(2)]

    def side_copy(i, stage):
        tensor, b = sides[i]
        return pltpu.make_async_remote_copy(
            src_ref=(side_send if stage == 0 else side_mid).at[tensor, b],
            dst_ref=(side_mid if stage == 0 else side_end).at[tensor, b],
            send_sem=y_sems.at[2 + stage, 0, i],
            recv_sem=y_sems.at[2 + stage, 1, i],
            device_id=place.far if stage == 0 else place.near,
            device_id_type=MESH,
        )

    for i, (tensor, b) in enumerate(sides):
        side_send[tensor, b] = side(tensor, 1, b).astype(BF16)
        side_copy(i, 0).start()

    hidden_all = hid_m[0] + hid_m[1]
    grad_all = gp_m[0] + gp_m[1]
    rank_start(
        two, 1, dot(grad_all, m_low[:, 0:hidden_dev], NT), dot(hidden_all, m_low[:, 0:hidden_dev], NT)
    )

    bufs = (
        (low_z1, low_x2, low_x1, low_z2),
        (up_z1, up_x2, up_x1, up_z2),
        (dn_z1, dn_x2, dn_x1, dn_z2),
    )
    terms = (t_low, t_up, t_down)
    scatters = [
        [
            Scatter(
                place, terms[i], kind, terms[i].shape[3] // 4,
                *(bufs[i][0:2] if kind < 2 else bufs[i][2:4]),
                rs_send.at[i], rs_recv.at[i],
            )
            for kind in range(4)
        ]
        for i in range(3)
    ]

    def scatter_step(i, k):
        for one_chunk in scatters[i]:
            one_chunk.advance(k)

    def shaped(value):
        return (value * scale).reshape(nx, nz, rows, value.shape[1]).astype(BF16)

    @pl.loop(0, hb)
    def _(h):
        home_h = home[h]
        for s in range(SLOTS):
            at = pl.ds(pl.multiple_of((s * hb + h) * blk, blk), blk)
            t_up[:, :, :, at] = shaped(dot(xt[s, home_h], gp[h]))

    scatter_step(1, 0)

    @pl.loop(0, hb)
    def _(h):
        home_h = home[h]
        for s in range(SLOTS):
            at = pl.ds(pl.multiple_of((s * hb + h) * blk, blk), blk)
            t_down[:, :, :, at] = shaped(dot(hid_t[h], gs[s, home_h]))

    scatter_step(2, 0)

    def side_pass(i):
        tensor, b = sides[i]
        own = side(tensor, 2, b)
        side_copy(i, 0).wait_recv()
        side_mid[tensor, b] = (side_mid[tensor, b].astype(F32) + own).astype(BF16)
        side_copy(i, 1).start()

    rank_in_t = rank_in.T
    rank_back_t = rank_back.T
    for j in range(hb):
        at = slice(j * blk, (j + 1) * blk)
        t_low[:, :, :, at] = shaped(
            dot(rank_in_t, grad_all[:, at]) + dot(rank_back_t, hidden_all[:, at])
        )
    scatter_step(1, 1)
    two.middle()
    side_pass(0)
    scatter_step(2, 1)
    scatter_step(1, 2)
    side_pass(1)
    two.end()
    rank2 = rank_two[...].reshape(tokens, blk)
    rank_grad = jnp.where(is_low, rank2, zero)
    rank_mid = jnp.where(is_low, zero, rank2)
    rank_grad_t = rank_grad.T
    rank_mid_t = rank_mid.T
    for j in range(2):
        at = slice(j * blk, (j + 1) * blk)
        to = slice(hidden_dev + j * blk, hidden_dev + (j + 1) * blk)
        t_low[:, :, :, to] = shaped(
            dot(rank_grad_t, x_ref[:, at]) + dot(rank_mid_t, g_ref[:, at])
        )
    scatter_step(0, 0)
    scatter_step(2, 2)
    scatter_step(1, 3)
    scatter_step(0, 1)
    side_pass(2)
    for k in range(3, rounds + 1):
        scatter_step(2, k)
        if k + 1 <= rounds:
            scatter_step(1, k + 1)
        scatter_step(0, k - 1)
        if k == 3:
            side_pass(3)
    scatter_step(0, rounds)

    for i, (tensor, b) in enumerate(sides):
        at = slice(b * blk, (b + 1) * blk)
        to = slice(hidden_dev + b * blk, hidden_dev + (b + 1) * blk)
        rank = rank_mid if tensor == 0 else rank_grad
        total = side(tensor, 0, b) + dot(rank, m_low[:, to])
        side_copy(i, 1).wait_recv()
        total = total + side_end[tensor, b].astype(F32)
        ref = out_ref if tensor == 0 else ig_ref
        ref[:, at] = total.astype(BF16)

    def whole(i):
        return jnp.concatenate([one_chunk.result for one_chunk in scatters[i]], axis=1)

    for i, ref in ((1, gbu_ref), (2, gbd_ref)):
        total = whole(i).astype(BF16)
        for s in range(SLOTS):
            for h in range(hb):
                at = (s * hb + h) * blk
                ref[h, s] = total[:, at : at + blk]
    low = whole(0)
    gur_ref[...] = low[:half, :hidden_dev].astype(BF16)
    gdl_ref[...] = low[half:, :hidden_dev].astype(BF16)
    gul_ref[...] = low[:half, hidden_dev:].astype(BF16)
    gdr_ref[...] = low[half:, hidden_dev:].astype(BF16)

    for i in range(3):
        for kind in range(4):
            gathers[i][kind].finish()
            scatters[i][kind].finish()
    for i in range(8):
        y_copy(i, 0).wait_send()
        y_copy(i, 1).wait_send()
    for i in range(4):
        side_copy(i, 0).wait_send()
        side_copy(i, 1).wait_send()
    one.finish()
    two.finish()


def per_device(
    nx, nz, nh,
    inputs, out_grad, home_block, blocks_up, blocks_down, up_left, up_right, down_left, down_right,
):
    tokens, width_dev = inputs.shape
    hb, slots, rows, blk = blocks_up.shape
    hidden_dev = hb * blk
    scale = float(nx * nz * tokens) ** (-0.5)
    low_cols, blk_cols = hidden_dev + width_dev, slots * hb * blk
    vmem = pl.BlockSpec(memory_space=pltpu.VMEM)
    smem = pl.BlockSpec(memory_space=pltpu.SMEM)

    def buf(shape, dtype=BF16):
        return pltpu.VMEM(shape, dtype)

    gathered = [buf((nx, nz, rows, c)) for c in (low_cols, blk_cols, blk_cols)]
    landing = []
    for c in (low_cols, blk_cols, blk_cols):
        w = c // 4
        landing += [
            buf((2, nz - 1, nx, rows, w)),
            buf((2, nx - 1, rows, w)),
            buf((2, nx - 1, nz, rows, w)),
            buf((2, nz - 1, rows, w)),
        ]
    ups = up_left.T, down_left.T
    outs = pl.pallas_call(
        functools.partial(layer, nx, nz, nh, scale),
        out_shape=[
            jax.ShapeDtypeStruct(a.shape, BF16)
            for a in (
                inputs, out_grad, blocks_up, blocks_down, ups[0], up_right, ups[1], down_right,
            )
        ],
        in_specs=[vmem, vmem, smem] + [vmem] * 6,
        out_specs=[vmem] * 8,
        scratch_shapes=gathered
        + gathered
        + landing
        + [
            buf((slots, blk, hidden_dev)),
            buf((slots, hidden_dev, blk)),
            buf((blk, low_cols)),
            buf((slots, 2, tokens, blk)),
            buf((slots, 2, tokens, blk)),
            buf((slots, 2, blk, tokens)),
            buf((8, 128), F32),
            buf((8, 128), F32),
            buf((hb, blk, tokens)),
            buf((hb, tokens, blk)),
            buf((2, tokens, hidden_dev)),
            buf((2, tokens, hidden_dev)),
            buf((2, nh, tokens // nh, blk)),
            buf((2, nh, tokens // nh, blk)),
            buf((nh, tokens // nh, blk)),
            buf((nh, tokens // nh, blk)),
            buf((2, 2, tokens, blk)),
            buf((2, 2, tokens, blk)),
            buf((2, 2, tokens, blk)),
            pltpu.SemaphoreType.DMA((3, 4, 4)),
            pltpu.SemaphoreType.DMA((3, 4, nx + nz - 2)),
            pltpu.SemaphoreType.DMA((3, 4, 4)),
            pltpu.SemaphoreType.DMA((3, 4, nx + nz - 2)),
            pltpu.SemaphoreType.DMA((2, 4, nh)),
            pltpu.SemaphoreType.DMA((4, 2, 8)),
        ],
        compiler_params=pltpu.CompilerParams(
            collective_id=0, has_side_effects=True, vmem_limit_bytes=60 * 2**20
        ),
    )(
        inputs, out_grad, home_block, blocks_up, blocks_down, ups[0], up_right, ups[1], down_right,
    )
    out, ig, gbu, gbd, gul, gur, gdl, gdr = outs
    return out, ig, gbu, gbd, gul.T, gur, gdl.T, gdr


def solution(mesh, nx=4):
    n_dp, nh = mesh.shape["dp"], mesh.shape["hid"]
    placed = (
        P("dp", "hid"),
        P("dp", "hid"),
        P("hid"),
        P("hid", None, "dp", None),
        P("hid", None, "dp", None),
        P("hid", "dp"),
        P("dp", "hid"),
        P("hid", "dp"),
        P("dp", "hid"),
    )
    return jax.shard_map(
        functools.partial(per_device, nx, n_dp // nx, nh),
        mesh=mesh,
        in_specs=placed,
        out_specs=(
            P("dp", "hid"),
            P("dp", "hid"),
            P("hid", None, "dp", None),
            P("hid", None, "dp", None),
            P("hid", "dp"),
            P("dp", "hid"),
            P("hid", "dp"),
            P("dp", "hid"),
        ),
        check_vma=False,
    )
```

```python
import functools

import jax
import jax.numpy as jnp
from jax import lax
from jax.experimental import pallas as pl
from jax.experimental.pallas import tpu as pltpu
from jax.sharding import PartitionSpec as P

MESH = pl.DeviceIdType.MESH
gelu_coef = 0.7978845608028654
cubic_coef = 0.044715
SLOTS = 3
F32 = jnp.float32
BF16 = jnp.bfloat16
NN = (((1,), (0,)), ((), ()))
NT = (((1,), (1,)), ((), ()))


def dot(a, b, dims=NN):
    return lax.dot_general(a, b, dims, preferred_element_type=F32)


def flip(index, bit):
    return index + bit - 2 * bit * lax.rem(lax.div(index, bit), 2)


def wrap(value, n):
    return lax.rem(value + 4 * n, n)


def gelu_pair(pre_act):
    tangent = jnp.tanh(gelu_coef * (pre_act + cubic_coef * pre_act * pre_act * pre_act))
    activated = 0.5 * pre_act * (1.0 + tangent)
    derivative = 0.5 * (1.0 + tangent) + 0.5 * pre_act * (1.0 - tangent * tangent) * gelu_coef * (
        1.0 + 3.0 * cubic_coef * pre_act * pre_act
    )
    return activated, derivative


class Place:
    def __init__(self, nx, nz, nh):
        self.size = {"x": nx, "z": nz}
        self.nh = nh
        self.dp = lax.axis_index("dp")
        self.hid = lax.axis_index("hid")
        self.pos = {"x": lax.div(self.dp, nz), "z": lax.rem(self.dp, nz)}
        self.near = (self.dp, flip(self.hid, nh // 4))
        self.far = (self.dp, flip(flip(self.hid, nh // 4), nh // 2))

    def neighbour(self, axis, o):
        x, z = self.pos["x"], self.pos["z"]
        if axis == "x":
            x = wrap(x + o, self.size["x"])
        else:
            z = wrap(z + o, self.size["z"])
        return (x * self.size["z"] + z, self.hid)

    def peer(self, j):
        return (self.dp, lax.rem(self.hid + j, self.nh))


def gather_axes(kind):
    return ("x", "z") if kind < 2 else ("z", "x")


def ring_dirs(n):
    return [(0, n // 2)] + ([(1, n // 2 - 1)] if n > 2 else [])


class TorusGather:
    def __init__(self, place, buf, kind, send_sem, recv_sem):
        self.place, self.buf, self.kind = place, buf, kind
        self.width = buf.shape[3] // 2
        self.axes = ("x", "z") if kind == 0 else ("z", "x")
        self.n = [place.size[a] for a in self.axes]
        self.send_sem, self.recv_sem = send_sem, recv_sem
        self.rounds = self.n[0] // 2 + self.n[1] // 2
        self.sent = []
        self.count = 0
        self.ids = {}

    def view(self, f, g, part):
        at = {}
        for axis, n, off in zip(self.axes, self.n, (f, g)):
            at[axis] = wrap(self.place.pos[axis] - off, n)
        first = self.kind * self.width
        width = self.width
        if part is not None:
            width = width // 2
            first = first + part * width
        return self.buf.at[at["x"], at["z"], :, pl.ds(first, width)]

    def copy(self, level, f, g, o, ref):
        at = self.ids.setdefault((level, f, g, o), len(self.ids))
        return pltpu.make_async_remote_copy(
            src_ref=ref,
            dst_ref=ref,
            send_sem=self.send_sem.at[self.kind, at],
            recv_sem=self.recv_sem.at[self.kind, at],
            device_id=self.place.neighbour(self.axes[level], o),
            device_id_type=MESH,
        )

    def send(self, level, f, g, o, part):
        made = self.copy(level, f, g, o, self.view(f, g, part))
        made.start()
        self.sent.append(made)

    def spread(self, level, f, g):
        here = f if level == 0 else g
        half = self.n[level] // 2
        for o in (1, -1):
            if here * o < 0 or abs(here) >= half:
                continue
            part = None if abs(here) + 1 < half else (0 if o > 0 else 1)
            self.send(level, f, g, o, part)

    def stops(self, level):
        half = self.n[level] // 2
        return [(0, 0)] + [(o * t, t) for t in range(1, half) for o in (1, -1)] + [(half, half)]

    def arrive(self, level, f, g):
        here = f if level == 0 else g
        half = self.n[level] // 2
        for o in (1, -1):
            if here * o < 0 and abs(here) < half:
                continue
            last = o * (abs(here) - 1)
            back = (last, g) if level == 0 else (f, last)
            part = None if abs(here) < half else (0 if o > 0 else 1)
            self.copy(level, *back, o, self.view(f, g, part)).wait_recv()

    def advance(self, k):
        for f, a in self.stops(0):
            if a == k:
                if a:
                    self.arrive(0, f, 0)
                self.spread(0, f, 0)
                self.spread(1, f, 0)
        for f, a in self.stops(0):
            for g, b in self.stops(1):
                if b and a + b == k:
                    self.arrive(1, f, g)
                    self.spread(1, f, g)

    def finish(self):
        for made in self.sent:
            made.wait_send()
        self.sent = []


class Scatter:
    def __init__(self, place, terms, kind, width, first_buf, second_buf, send_sem, recv_sem):
        self.place, self.terms, self.kind = place, terms, kind
        self.columns = pl.ds(kind * width, width)
        self.bufs = (first_buf, second_buf)
        self.send_sem, self.recv_sem = send_sem, recv_sem
        self.axes = gather_axes(kind)[::-1]
        self.turns = [place.size[a] // 2 for a in self.axes]
        self.rounds = sum(self.turns)
        self.sent = {}

    def term(self, phase, at):
        axis = self.axes[phase]
        own = self.place.pos
        if phase == 1:
            x, z = (at, own["z"]) if axis == "x" else (own["x"], at)
            return self.terms.at[x, z, :, self.columns]
        if axis == "x":
            return self.terms.at[at, :, :, self.columns]
        return self.terms.at[:, at, :, self.columns]

    def slot(self, phase, d, t):
        n = self.place.size[self.axes[phase]]
        return (n // 2 if d else 0) + t - 1

    def arrived(self, phase, d, t):
        return self.bufs[phase].at[self.kind % 2, self.slot(phase, d, t)]

    def o(self, d):
        return (1 if self.kind % 2 == 0 else -1) * (1 if d == 0 else -1)

    def copy(self, phase, d, t, source):
        axis = self.axes[phase]
        first = 0 if phase == 0 else self.place.size[self.axes[0]] - 1
        return pltpu.make_async_remote_copy(
            src_ref=source,
            dst_ref=self.arrived(phase, d, t),
            send_sem=self.send_sem.at[self.kind, phase * 2 + d],
            recv_sem=self.recv_sem.at[self.kind, first + self.slot(phase, d, t)],
            device_id=self.place.neighbour(axis, self.o(d)),
            device_id_type=MESH,
        )

    def send(self, phase, d, t, source):
        before = self.sent.pop((phase, d), None)
        if before is not None:
            before.wait_send()
        made = self.copy(phase, d, t, source)
        made.start()
        self.sent[(phase, d)] = made

    def dest(self, phase, d, t, count):
        axis = self.axes[phase]
        return wrap(self.place.pos[axis] + self.o(d) * (count - t + 1), self.place.size[axis])

    def begin(self, phase):
        for d, count in ring_dirs(self.place.size[self.axes[phase]]):
            self.send(phase, d, 1, self.term(phase, self.dest(phase, d, 1, count)))

    def advance(self, k):
        if k == 0:
            self.begin(0)
            return
        phase = 0 if k <= self.turns[0] else 1
        t = k - (self.turns[0] if phase else 0)
        axis = self.axes[phase]
        dirs = ring_dirs(self.place.size[axis])
        for d, count in dirs:
            if t <= count:
                held = self.arrived(phase, d, t)
                self.copy(phase, d, t, held).wait_recv()
                if t < count:
                    held[...] = held[...] + self.term(phase, self.dest(phase, d, t + 1, count))[...]
                    self.send(phase, d, t + 1, held)
        if t == self.turns[phase]:
            own = self.term(phase, self.place.pos[axis])
            total = own[...].astype(F32)
            for d, count in dirs:
                total = total + self.arrived(phase, d, count)[...].astype(F32)
            if phase == 0:
                own[...] = total.astype(BF16)
                self.begin(1)
            else:
                self.result = total

    def finish(self):
        for made in self.sent.values():
            made.wait_send()
        self.sent = {}


class DirectGather:
    def __init__(self, place, buf, sems):
        self.place, self.buf, self.sems = place, buf, sems

    def copies(self, phase, sending):
        place = self.place
        axis = "xz"[phase]
        n = place.size[axis]
        made = []
        for j in range(1, n):
            if phase == 0:
                at = place.pos["x"] if sending else wrap(place.pos["x"] - j, n)
                ref = self.buf.at[at, place.pos["z"]]
            else:
                at = place.pos["z"] if sending else wrap(place.pos["z"] - j, n)
                ref = self.buf.at[:, at]
            made.append(
                pltpu.make_async_remote_copy(
                    src_ref=ref,
                    dst_ref=ref,
                    send_sem=self.sems.at[0, phase, j],
                    recv_sem=self.sems.at[1, phase, j],
                    device_id=place.neighbour(axis, j),
                    device_id_type=MESH,
                )
            )
        return made

    def begin(self, phase):
        for made in self.copies(phase, True):
            made.start()

    def wait(self, phase):
        for made in self.copies(phase, False):
            made.wait_recv()

    def finish(self):
        for phase in range(2):
            for made in self.copies(phase, True):
                made.wait_send()


class DirectScatter:
    def __init__(self, place, terms, first_buf, second_buf, sems):
        self.place, self.terms, self.sems = place, terms, sems
        self.bufs = (first_buf, second_buf)

    def term(self, phase, at):
        if phase == 0:
            return self.terms.at[:, at]
        return self.terms.at[at, self.place.pos["z"]]

    def copies(self, phase):
        place = self.place
        axis = "zx"[phase]
        n = place.size[axis]
        return [
            pltpu.make_async_remote_copy(
                src_ref=self.term(phase, wrap(place.pos[axis] + j, n)),
                dst_ref=self.bufs[phase].at[j],
                send_sem=self.sems.at[0, phase, j],
                recv_sem=self.sems.at[1, phase, j],
                device_id=place.neighbour(axis, j),
                device_id_type=MESH,
            )
            for j in range(1, n)
        ]

    def begin(self, phase):
        for made in self.copies(phase):
            made.start()

    def wait(self, phase):
        axis = "zx"[phase]
        for made in self.copies(phase):
            made.wait_recv()
        own = self.term(phase, self.place.pos[axis])
        total = own[...].astype(F32)
        for j in range(1, self.place.size[axis]):
            total = total + self.bufs[phase][j].astype(F32)
        if phase == 0:
            own[...] = total.astype(BF16)
        else:
            self.result = total

    def finish(self):
        for phase in range(2):
            for made in self.copies(phase):
                made.wait_send()


class RankSum:
    def __init__(self, place, parts, arrived, whole, sems):
        self.place, self.parts, self.got, self.whole, self.sems = place, parts, arrived, whole, sems

    def scatter_copy(self, j):
        peer = self.place.peer(j)
        return pltpu.make_async_remote_copy(
            src_ref=self.parts.at[peer[1]],
            dst_ref=self.got.at[j],
            send_sem=self.sems.at[0, j],
            recv_sem=self.sems.at[1, j],
            device_id=peer,
            device_id_type=MESH,
        )

    def gather_copy(self, j, at):
        return pltpu.make_async_remote_copy(
            src_ref=self.whole.at[at],
            dst_ref=self.whole.at[at],
            send_sem=self.sems.at[2, j],
            recv_sem=self.sems.at[3, j],
            device_id=self.place.peer(j),
            device_id_type=MESH,
        )

    def each(self, body):
        @pl.loop(1, self.place.nh)
        def _(j):
            body(j)

    def start(self):
        self.each(lambda j: self.scatter_copy(j).start())

    def middle(self):
        self.each(lambda j: self.scatter_copy(j).wait_recv())
        me = self.place.hid
        total = self.parts[me].astype(F32)
        for j in range(1, self.place.nh):
            total = total + self.got[j].astype(F32)
        self.whole[me] = total.astype(BF16)
        self.each(lambda j: self.gather_copy(j, me).start())

    def end(self):
        nh = self.place.nh

        def wait(j):
            self.gather_copy(j, lax.rem(self.place.hid + nh - j, nh)).wait_recv()

        self.each(wait)

    def finish(self):
        def wait(j):
            self.scatter_copy(j).wait_send()
            self.gather_copy(j, self.place.hid).wait_send()

        self.each(wait)


def layer(
    nx, nz, nh, scale,
    x_ref, g_ref, home, bu_ref, bd_ref, ul_ref, ur_ref, dl_ref, dr_ref,
    out_ref, ig_ref, gbu_ref, gbd_ref, gul_ref, gur_ref, gdl_ref, gdr_ref,
    g_low, g_all, t_low, t_all,
    low_first, low_second, all_z1, all_x2, all_x1, all_z2,
    w_up, w_down, m_one, m_two, xs, gs, xt, hid_t, gp, hid_m, gp_m,
    rank_parts, rank_got, rank_one, rank_two,
    side_send, side_mid, side_end,
    ag_send, ag_recv, rs_send, rs_recv, rank_sems, low_sems, y_sems,
):
    place = Place(nx, nz, nh)
    rows, blk = bu_ref.shape[2], bu_ref.shape[3]
    tokens = x_ref.shape[0]
    hb = bu_ref.shape[0]
    half = rows // 2
    px, pz = place.pos["x"], place.pos["z"]

    barrier = pltpu.get_barrier_semaphore()
    for axis in ("x", "z"):
        for o in range(1, place.size[axis]):
            pl.semaphore_signal(barrier, inc=1, device_id=place.neighbour(axis, o), device_id_type=MESH)

    @pl.loop(1, nh)
    def _(j):
        pl.semaphore_signal(barrier, inc=1, device_id=place.peer(j), device_id_type=MESH)

    hidden_dev, width_dev = ur_ref.shape[1], dr_ref.shape[1]
    g_low[px, pz] = jnp.concatenate([ul_ref[...].astype(F32), dr_ref[...].astype(F32)], axis=0).astype(BF16)
    downs = SLOTS * hb * blk
    ranks = 2 * downs
    g_all[px, pz, :, ranks:] = jnp.concatenate(
        [ur_ref[...].astype(F32), dl_ref[...].astype(F32)], axis=0
    ).astype(BF16)
    for s in range(SLOTS):
        for h in range(hb):
            at = (s * hb + h) * blk
            g_all[px, pz, :, at : at + blk] = bu_ref[h, s]
            g_all[px, pz, :, downs + at : downs + at + blk] = bd_ref[h, s]
    for b in range(2):
        xs[0, b] = x_ref[:, b * blk : (b + 1) * blk]
        gs[0, b] = g_ref[:, b * blk : (b + 1) * blk]
    pl.semaphore_wait(barrier, nx + nz + nh - 3)

    gathers = [TorusGather(place, g_all, kind, ag_send, ag_recv) for kind in range(2)]
    low_gather = DirectGather(place, g_low, low_sems.at[0])
    rounds = nx // 2 + nz // 2

    def gather_step(k):
        for one_half in gathers:
            one_half.advance(k)

    part = tokens // 2
    pieces = [(ref, b, q) for ref in (xs, gs) for b in range(2) for q in range(2)]

    def y_copy(i, stage):
        ref, b, q = pieces[i]
        at = pl.ds(q * part, part)
        return pltpu.make_async_remote_copy(
            src_ref=ref.at[0 if stage == 0 else 2, b, at],
            dst_ref=ref.at[2 if stage == 0 else 1, b, at],
            send_sem=y_sems.at[stage, 0, i],
            recv_sem=y_sems.at[stage, 1, i],
            device_id=place.near if stage == 0 else place.far,
            device_id_type=MESH,
        )

    def pass_on(i):
        y_copy(i, 0).wait_recv()
        y_copy(i, 1).start()

    column = lax.broadcasted_iota(jnp.int32, (tokens, blk), 1)
    is_low = lax.rem(column, rows) < half

    def flat(buf, at, width):
        return buf[:, :, :, at : at + width].astype(F32).reshape(blk, width).astype(BF16)

    one = RankSum(place, rank_parts.at[0], rank_got.at[0], rank_one, rank_sems.at[0])
    two = RankSum(place, rank_parts.at[1], rank_got.at[1], rank_two, rank_sems.at[1])

    def rank_start(which, index, low, high):
        mixed = jnp.where(is_low, low, high).reshape(nh, tokens // nh, blk)
        rank_parts[index] = mixed.astype(BF16)
        which.start()

    low_gather.begin(0)
    gather_step(0)
    for i in range(4):
        y_copy(i, 0).start()
    low_gather.wait(0)
    low_gather.begin(1)
    gather_step(1)
    for i in range(4, 8):
        y_copy(i, 0).start()
    pass_on(0)
    gather_step(2)
    low_gather.wait(1)
    for j in range(2):
        m_two[:, j * blk : (j + 1) * blk] = flat(g_low, j * blk, blk)
    rank_start(one, 0, dot(x_ref[...], m_two[...], NT), dot(g_ref[...], m_two[...], NT))
    pass_on(1)
    pass_on(2)
    gather_step(3)
    pass_on(3)
    pass_on(4)
    gather_step(4)
    one.middle()
    pass_on(5)
    gather_step(5)
    pass_on(6)
    pass_on(7)
    for i in range(4):
        y_copy(i, 1).wait_recv()
    for s in range(SLOTS):
        for b in range(2):
            xt[s, b] = xs[s, b].T
    one.end()
    for k in range(6, rounds + 1):
        gather_step(k)
    for j in range(SLOTS * hb):
        w_up[j // hb, :, (j % hb) * blk : (j % hb + 1) * blk] = flat(g_all, j * blk, blk)
        w_down[j // hb, (j % hb) * blk : (j % hb + 1) * blk, :] = flat(g_all, downs + j * blk, blk)
    for j in range(hb):
        m_one[:, j * blk : (j + 1) * blk] = flat(g_all, ranks + j * blk, blk)
    for i in range(4, 8):
        y_copy(i, 1).wait_recv()

    rank1 = rank_one[...].reshape(tokens, blk)
    zero = jnp.zeros_like(rank1)
    rank_in = jnp.where(is_low, rank1, zero)
    rank_back = jnp.where(is_low, zero, rank1)

    @pl.loop(0, hb)
    def _(h):
        home_h = home[h]
        at = pl.ds(pl.multiple_of(h * blk, blk), blk)
        value = dot(rank_in, m_one[:, at])
        grad = dot(rank_back, m_one[:, at])
        for s in range(SLOTS):
            value = value + dot(xs[s, home_h], w_up[s, :, at])
            grad = grad + dot(gs[s, home_h], w_down[s, at, :], NT)
        activated, derivative = gelu_pair(value)
        hidden = activated.astype(BF16)
        grad_pre = (grad * derivative).astype(BF16)
        hid_t[h] = hidden.T
        gp[h] = grad_pre
        for b in range(2):
            keep = jnp.where(home_h == b, 1.0, 0.0).astype(F32)
            hid_m[b, :, at] = (hidden.astype(F32) * keep).astype(BF16)
            gp_m[b, :, at] = (grad_pre.astype(F32) * keep).astype(BF16)

    def side(tensor, s, b):
        if tensor == 0:
            return dot(hid_m[b], w_down[s])
        return dot(gp_m[b], w_up[s], NT)

    sides = [(tensor, b) for tensor in range(2) for b in range(2)]

    def side_copy(i, stage):
        tensor, b = sides[i]
        return pltpu.make_async_remote_copy(
            src_ref=(side_send if stage == 0 else side_mid).at[tensor, b],
            dst_ref=(side_mid if stage == 0 else side_end).at[tensor, b],
            send_sem=y_sems.at[2 + stage, 0, i],
            recv_sem=y_sems.at[2 + stage, 1, i],
            device_id=place.far if stage == 0 else place.near,
            device_id_type=MESH,
        )

    hidden_all = hid_m[0] + hid_m[1]
    grad_all = gp_m[0] + gp_m[1]
    rank_start(
        two, 1, dot(grad_all, m_one[...], NT), dot(hidden_all, m_one[...], NT)
    )
    for i, (tensor, b) in enumerate(sides):
        side_send[tensor, b] = side(tensor, 1, b).astype(BF16)
        side_copy(i, 0).start()

    scatters = [
        Scatter(
            place, t_all, kind, t_all.shape[3] // 4,
            *((all_z1, all_x2) if kind < 2 else (all_x1, all_z2)),
            rs_send, rs_recv,
        )
        for kind in range(4)
    ]
    low_scatter = DirectScatter(place, t_low, low_first, low_second, low_sems.at[1])

    def scatter_step(k):
        for one_chunk in scatters:
            one_chunk.advance(k)

    def shaped(value):
        return (value * scale).reshape(nx, nz, rows, value.shape[1]).astype(BF16)

    @pl.loop(0, hb)
    def _(h):
        home_h = home[h]
        for s in range(SLOTS):
            at = pl.ds(pl.multiple_of((s * hb + h) * blk, blk), blk)
            t_all[:, :, :, at] = shaped(dot(xt[s, home_h], gp[h]))
            at = pl.ds(pl.multiple_of(downs + (s * hb + h) * blk, blk), blk)
            t_all[:, :, :, at] = shaped(dot(hid_t[h], gs[s, home_h]))

    rank_in_t = rank_in.T
    rank_back_t = rank_back.T
    for j in range(hb):
        at = slice(j * blk, (j + 1) * blk)
        t_all[:, :, :, ranks + j * blk : ranks + (j + 1) * blk] = shaped(
            dot(rank_in_t, grad_all[:, at]) + dot(rank_back_t, hidden_all[:, at])
        )
    scatter_step(0)

    def side_pass(i):
        tensor, b = sides[i]
        own = side(tensor, 2, b)
        side_copy(i, 0).wait_recv()
        side_mid[tensor, b] = (side_mid[tensor, b].astype(F32) + own).astype(BF16)
        side_copy(i, 1).start()

    two.middle()
    scatter_step(1)
    side_pass(0)
    two.end()
    rank2 = rank_two[...].reshape(tokens, blk)
    rank_grad = jnp.where(is_low, rank2, zero)
    rank_mid = jnp.where(is_low, zero, rank2)
    rank_grad_t = rank_grad.T
    rank_mid_t = rank_mid.T
    for j in range(2):
        at = slice(j * blk, (j + 1) * blk)
        t_low[:, :, :, at] = shaped(dot(rank_grad_t, x_ref[:, at]) + dot(rank_mid_t, g_ref[:, at]))
    low_scatter.begin(0)

    def result(i):
        tensor, b = sides[i]
        at = slice(b * blk, (b + 1) * blk)
        rank = rank_mid if tensor == 0 else rank_grad
        total = side(tensor, 0, b) + dot(rank, m_two[:, at])
        side_copy(i, 1).wait_recv()
        total = total + side_end[tensor, b].astype(F32)
        ref = out_ref if tensor == 0 else ig_ref
        ref[:, at] = total.astype(BF16)

    scatter_step(2)
    side_pass(1)
    scatter_step(3)
    side_pass(2)
    low_scatter.wait(0)
    low_scatter.begin(1)
    result(0)
    scatter_step(4)
    side_pass(3)
    result(1)
    scatter_step(5)
    low_scatter.wait(1)
    low = low_scatter.result
    gul_ref[...] = low[:half].astype(BF16)
    gdr_ref[...] = low[half:].astype(BF16)
    result(2)
    for k in range(6, rounds + 1):
        scatter_step(k)
    result(3)

    total = jnp.concatenate([one_chunk.result for one_chunk in scatters], axis=1)
    for first, ref in ((0, gbu_ref), (downs, gbd_ref)):
        for s in range(SLOTS):
            for h in range(hb):
                at = first + (s * hb + h) * blk
                ref[h, s] = total[:, at : at + blk].astype(BF16)
    gur_ref[...] = total[:half, ranks:].astype(BF16)
    gdl_ref[...] = total[half:, ranks:].astype(BF16)

    for one_chunk in gathers + scatters + [low_gather, low_scatter]:
        one_chunk.finish()
    for i in range(8):
        y_copy(i, 0).wait_send()
        y_copy(i, 1).wait_send()
    for i in range(4):
        side_copy(i, 0).wait_send()
        side_copy(i, 1).wait_send()
    one.finish()
    two.finish()


def hand_over(*refs):
    n = len(refs) // 2
    for source, target in zip(refs[:n], refs[n:]):
        target[...] = source[...]


def per_device(
    nx, nz, nh,
    inputs, out_grad, home_block, blocks_up, blocks_down, up_left, up_right, down_left, down_right,
):
    tokens, width_dev = inputs.shape
    hb, slots, rows, blk = blocks_up.shape
    hidden_dev = hb * blk
    scale = float(nx * nz * tokens) ** (-0.5)
    all_cols = 2 * slots * hb * blk + hidden_dev
    vmem = pl.BlockSpec(memory_space=pltpu.VMEM)
    smem = pl.BlockSpec(memory_space=pltpu.SMEM)

    def buf(shape, dtype=BF16):
        return pltpu.VMEM(shape, dtype)

    gathered = [buf((nx, nz, rows, c)) for c in (width_dev, all_cols)]
    w = all_cols // 4
    landing = [
        buf((nz, nx, rows, width_dev)),
        buf((nx, rows, width_dev)),
        buf((2, nz - 1, nx, rows, w)),
        buf((2, nx - 1, rows, w)),
        buf((2, nx - 1, nz, rows, w)),
        buf((2, nz - 1, rows, w)),
    ]
    ups = up_left.T, down_left.T
    outs = pl.pallas_call(
        functools.partial(layer, nx, nz, nh, scale),
        out_shape=[
            jax.ShapeDtypeStruct(a.shape, BF16)
            for a in (
                inputs, out_grad, blocks_up, blocks_down, ups[0], up_right, ups[1], down_right,
            )
        ],
        in_specs=[vmem, vmem, smem] + [vmem] * 6,
        out_specs=[vmem] * 8,
        scratch_shapes=gathered
        + gathered
        + landing
        + [
            buf((slots, blk, hidden_dev)),
            buf((slots, hidden_dev, blk)),
            buf((blk, hidden_dev)),
            buf((blk, width_dev)),
            buf((slots, 2, tokens, blk)),
            buf((slots, 2, tokens, blk)),
            buf((slots, 2, blk, tokens)),
            buf((hb, blk, tokens)),
            buf((hb, tokens, blk)),
            buf((2, tokens, hidden_dev)),
            buf((2, tokens, hidden_dev)),
            buf((2, nh, tokens // nh, blk)),
            buf((2, nh, tokens // nh, blk)),
            buf((nh, tokens // nh, blk)),
            buf((nh, tokens // nh, blk)),
            buf((2, 2, tokens, blk)),
            buf((2, 2, tokens, blk)),
            buf((2, 2, tokens, blk)),
            pltpu.SemaphoreType.DMA((2, max(nx, nz) * (min(nx, nz) + 1))),
            pltpu.SemaphoreType.DMA((2, max(nx, nz) * (min(nx, nz) + 1))),
            pltpu.SemaphoreType.DMA((4, 4)),
            pltpu.SemaphoreType.DMA((4, nx + nz - 2)),
            pltpu.SemaphoreType.DMA((2, 4, nh)),
            pltpu.SemaphoreType.DMA((2, 2, 2, max(nx, nz))),
            pltpu.SemaphoreType.DMA((4, 2, 8)),
        ],
        compiler_params=pltpu.CompilerParams(
            collective_id=0, has_side_effects=True, vmem_limit_bytes=60 * 2**20
        ),
    )(
        inputs, out_grad, home_block, blocks_up, blocks_down, ups[0], up_right, ups[1], down_right,
    )
    out, ig, gbu, gbd, gul, gur, gdl, gdr = pl.pallas_call(
        hand_over,
        out_shape=[jax.ShapeDtypeStruct(a.shape, a.dtype) for a in outs],
        in_specs=[vmem] * len(outs),
        out_specs=[vmem] * len(outs),
    )(*outs)
    return out, ig, gbu, gbd, gul.T, gur, gdl.T, gdr


def solution(mesh, nx=4):
    n_dp, nh = mesh.shape["dp"], mesh.shape["hid"]
    placed = (
        P("dp", "hid"),
        P("dp", "hid"),
        P("hid"),
        P("hid", None, "dp", None),
        P("hid", None, "dp", None),
        P("hid", "dp"),
        P("dp", "hid"),
        P("hid", "dp"),
        P("dp", "hid"),
    )
    return jax.shard_map(
        functools.partial(per_device, nx, n_dp // nx, nh),
        mesh=mesh,
        in_specs=placed,
        out_specs=(
            P("dp", "hid"),
            P("dp", "hid"),
            P("hid", None, "dp", None),
            P("hid", None, "dp", None),
            P("hid", "dp"),
            P("dp", "hid"),
            P("hid", "dp"),
            P("dp", "hid"),
        ),
        check_vma=False,
    )
```

```python
import functools

import jax
import jax.numpy as jnp
from jax import lax
from jax.experimental import pallas as pl
from jax.experimental.pallas import tpu as pltpu
from jax.sharding import PartitionSpec as P

MESH = pl.DeviceIdType.MESH
gelu_coef = 0.7978845608028654
cubic_coef = 0.044715
SLOTS = 3
F32 = jnp.float32
BF16 = jnp.bfloat16
NN = (((1,), (0,)), ((), ()))
NT = (((1,), (1,)), ((), ()))


def dot(a, b, dims=NN):
    return lax.dot_general(a, b, dims, preferred_element_type=F32)


def flip(index, bit):
    return index + bit - 2 * bit * lax.rem(lax.div(index, bit), 2)


def wrap(value, n):
    return lax.rem(value + 4 * n, n)


def gelu_pair(pre_act):
    tangent = jnp.tanh(gelu_coef * (pre_act + cubic_coef * pre_act * pre_act * pre_act))
    activated = 0.5 * pre_act * (1.0 + tangent)
    derivative = 0.5 * (1.0 + tangent) + 0.5 * pre_act * (1.0 - tangent * tangent) * gelu_coef * (
        1.0 + 3.0 * cubic_coef * pre_act * pre_act
    )
    return activated, derivative


class Place:
    def __init__(self, nx, nz, nh):
        self.size = {"x": nx, "z": nz}
        self.nh = nh
        self.dp = lax.axis_index("dp")
        self.hid = lax.axis_index("hid")
        self.pos = {"x": lax.div(self.dp, nz), "z": lax.rem(self.dp, nz)}
        self.near = (self.dp, flip(self.hid, nh // 4))
        self.far = (self.dp, flip(flip(self.hid, nh // 4), nh // 2))

    def neighbour(self, axis, o):
        x, z = self.pos["x"], self.pos["z"]
        if axis == "x":
            x = wrap(x + o, self.size["x"])
        else:
            z = wrap(z + o, self.size["z"])
        return (x * self.size["z"] + z, self.hid)

    def peer(self, j):
        return (self.dp, lax.rem(self.hid + j, self.nh))


def gather_axes(kind):
    return ("x", "z") if kind < 2 else ("z", "x")


def ring_dirs(n):
    return [(0, n // 2)] + ([(1, n // 2 - 1)] if n > 2 else [])


def scatter_widths(total):
    return [11 * total // 56] * 2 + [17 * total // 56] * 2


class TorusGather:
    def __init__(self, place, buf, kind, send_sem, recv_sem):
        self.place, self.buf, self.kind = place, buf, kind
        total = buf.shape[3]
        self.first, self.width = ((0, 11 * total // 28), (11 * total // 28, 17 * total // 28))[kind]
        self.axes = ("x", "z") if kind == 0 else ("z", "x")
        self.n = [place.size[a] for a in self.axes]
        self.send_sem, self.recv_sem = send_sem, recv_sem
        self.rounds = self.n[0] // 2 + self.n[1] // 2
        self.sent = []
        self.count = 0
        self.ids = {}

    def view(self, f, g, part):
        at = {}
        for axis, n, off in zip(self.axes, self.n, (f, g)):
            at[axis] = wrap(self.place.pos[axis] - off, n)
        first, width = self.first, self.width
        if part is not None:
            width = width // 2
            first = first + part * width
        return self.buf.at[at["x"], at["z"], :, pl.ds(first, width)]

    def copy(self, level, f, g, o, ref):
        at = self.ids.setdefault((level, f, g, o), len(self.ids))
        return pltpu.make_async_remote_copy(
            src_ref=ref,
            dst_ref=ref,
            send_sem=self.send_sem.at[self.kind, at],
            recv_sem=self.recv_sem.at[self.kind, at],
            device_id=self.place.neighbour(self.axes[level], o),
            device_id_type=MESH,
        )

    def send(self, level, f, g, o, part):
        made = self.copy(level, f, g, o, self.view(f, g, part))
        made.start()
        self.sent.append(made)

    def spread(self, level, f, g):
        here = f if level == 0 else g
        half = self.n[level] // 2
        for o in (1, -1):
            if here * o < 0 or abs(here) >= half:
                continue
            part = None if abs(here) + 1 < half else (0 if o > 0 else 1)
            self.send(level, f, g, o, part)

    def stops(self, level):
        half = self.n[level] // 2
        return [(0, 0)] + [(o * t, t) for t in range(1, half) for o in (1, -1)] + [(half, half)]

    def arrive(self, level, f, g):
        here = f if level == 0 else g
        half = self.n[level] // 2
        for o in (1, -1):
            if here * o < 0 and abs(here) < half:
                continue
            last = o * (abs(here) - 1)
            back = (last, g) if level == 0 else (f, last)
            part = None if abs(here) < half else (0 if o > 0 else 1)
            self.copy(level, *back, o, self.view(f, g, part)).wait_recv()

    def advance(self, k):
        for f, a in self.stops(0):
            if a == k:
                if a:
                    self.arrive(0, f, 0)
                self.spread(0, f, 0)
                self.spread(1, f, 0)
        for f, a in self.stops(0):
            for g, b in self.stops(1):
                if b and a + b == k:
                    self.arrive(1, f, g)
                    self.spread(1, f, g)

    def finish(self):
        for made in self.sent:
            made.wait_send()
        self.sent = []


class Scatter:
    def __init__(self, place, terms, kind, widths, first_buf, second_buf, send_sem, recv_sem):
        self.place, self.terms, self.kind = place, terms, kind
        first = sum(widths[:kind])
        self.columns = pl.ds(first, widths[kind])
        self.bufs = (first_buf, second_buf)
        self.send_sem, self.recv_sem = send_sem, recv_sem
        self.axes = gather_axes(kind)[::-1]
        self.turns = [place.size[a] // 2 for a in self.axes]
        self.rounds = sum(self.turns)
        self.sent = {}

    def term(self, phase, at):
        axis = self.axes[phase]
        own = self.place.pos
        if phase == 1:
            x, z = (at, own["z"]) if axis == "x" else (own["x"], at)
            return self.terms.at[x, z, :, self.columns]
        if axis == "x":
            return self.terms.at[at, :, :, self.columns]
        return self.terms.at[:, at, :, self.columns]

    def slot(self, phase, d, t):
        n = self.place.size[self.axes[phase]]
        return (n // 2 if d else 0) + t - 1

    def arrived(self, phase, d, t):
        return self.bufs[phase].at[self.kind % 2, self.slot(phase, d, t)]

    def o(self, d):
        return (1 if self.kind % 2 == 0 else -1) * (1 if d == 0 else -1)

    def copy(self, phase, d, t, source):
        axis = self.axes[phase]
        first = 0 if phase == 0 else self.place.size[self.axes[0]] - 1
        return pltpu.make_async_remote_copy(
            src_ref=source,
            dst_ref=self.arrived(phase, d, t),
            send_sem=self.send_sem.at[self.kind, phase * 2 + d],
            recv_sem=self.recv_sem.at[self.kind, first + self.slot(phase, d, t)],
            device_id=self.place.neighbour(axis, self.o(d)),
            device_id_type=MESH,
        )

    def send(self, phase, d, t, source):
        before = self.sent.pop((phase, d), None)
        if before is not None:
            before.wait_send()
        made = self.copy(phase, d, t, source)
        made.start()
        self.sent[(phase, d)] = made

    def dest(self, phase, d, t, count):
        axis = self.axes[phase]
        return wrap(self.place.pos[axis] + self.o(d) * (count - t + 1), self.place.size[axis])

    def begin(self, phase):
        for d, count in ring_dirs(self.place.size[self.axes[phase]]):
            self.send(phase, d, 1, self.term(phase, self.dest(phase, d, 1, count)))

    def advance(self, k):
        if k == 0:
            self.begin(0)
            return
        phase = 0 if k <= self.turns[0] else 1
        t = k - (self.turns[0] if phase else 0)
        axis = self.axes[phase]
        dirs = ring_dirs(self.place.size[axis])
        for d, count in dirs:
            if t <= count:
                held = self.arrived(phase, d, t)
                self.copy(phase, d, t, held).wait_recv()
                if t < count:
                    held[...] = held[...] + self.term(phase, self.dest(phase, d, t + 1, count))[...]
                    self.send(phase, d, t + 1, held)
        if t == self.turns[phase]:
            own = self.term(phase, self.place.pos[axis])
            total = own[...].astype(F32)
            for d, count in dirs:
                total = total + self.arrived(phase, d, count)[...].astype(F32)
            if phase == 0:
                own[...] = total.astype(BF16)
                self.begin(1)
            else:
                self.result = total

    def finish(self):
        for made in self.sent.values():
            made.wait_send()
        self.sent = {}


class DirectGather:
    def __init__(self, place, buf, sems):
        self.place, self.buf, self.sems = place, buf, sems

    def copies(self, phase, sending):
        place = self.place
        axis = "xz"[phase]
        n = place.size[axis]
        made = []
        for j in range(1, n):
            if phase == 0:
                at = place.pos["x"] if sending else wrap(place.pos["x"] - j, n)
                ref = self.buf.at[at, place.pos["z"]]
            else:
                at = place.pos["z"] if sending else wrap(place.pos["z"] - j, n)
                ref = self.buf.at[:, at]
            made.append(
                pltpu.make_async_remote_copy(
                    src_ref=ref,
                    dst_ref=ref,
                    send_sem=self.sems.at[0, phase, j],
                    recv_sem=self.sems.at[1, phase, j],
                    device_id=place.neighbour(axis, j),
                    device_id_type=MESH,
                )
            )
        return made

    def begin(self, phase):
        for made in self.copies(phase, True):
            made.start()

    def wait(self, phase):
        for made in self.copies(phase, False):
            made.wait_recv()

    def finish(self):
        for phase in range(2):
            for made in self.copies(phase, True):
                made.wait_send()


class DirectScatter:
    def __init__(self, place, terms, first_buf, second_buf, sems):
        self.place, self.terms, self.sems = place, terms, sems
        self.bufs = (first_buf, second_buf)

    def term(self, phase, at):
        if phase == 0:
            return self.terms.at[:, at]
        return self.terms.at[at, self.place.pos["z"]]

    def copies(self, phase):
        place = self.place
        axis = "zx"[phase]
        n = place.size[axis]
        return [
            pltpu.make_async_remote_copy(
                src_ref=self.term(phase, wrap(place.pos[axis] + j, n)),
                dst_ref=self.bufs[phase].at[j],
                send_sem=self.sems.at[0, phase, j],
                recv_sem=self.sems.at[1, phase, j],
                device_id=place.neighbour(axis, j),
                device_id_type=MESH,
            )
            for j in range(1, n)
        ]

    def begin(self, phase):
        for made in self.copies(phase):
            made.start()

    def wait(self, phase):
        axis = "zx"[phase]
        for made in self.copies(phase):
            made.wait_recv()
        own = self.term(phase, self.place.pos[axis])
        total = own[...].astype(F32)
        for j in range(1, self.place.size[axis]):
            total = total + self.bufs[phase][j].astype(F32)
        if phase == 0:
            own[...] = total.astype(BF16)
        else:
            self.result = total

    def finish(self):
        for phase in range(2):
            for made in self.copies(phase):
                made.wait_send()


class RankSum:
    def __init__(self, place, parts, arrived, whole, sems):
        self.place, self.parts, self.got, self.whole, self.sems = place, parts, arrived, whole, sems

    def scatter_copy(self, j):
        peer = self.place.peer(j)
        return pltpu.make_async_remote_copy(
            src_ref=self.parts.at[peer[1]],
            dst_ref=self.got.at[j],
            send_sem=self.sems.at[0, j],
            recv_sem=self.sems.at[1, j],
            device_id=peer,
            device_id_type=MESH,
        )

    def gather_copy(self, j, at):
        return pltpu.make_async_remote_copy(
            src_ref=self.whole.at[at],
            dst_ref=self.whole.at[at],
            send_sem=self.sems.at[2, j],
            recv_sem=self.sems.at[3, j],
            device_id=self.place.peer(j),
            device_id_type=MESH,
        )

    def each(self, body):
        @pl.loop(1, self.place.nh)
        def _(j):
            body(j)

    def start(self):
        self.each(lambda j: self.scatter_copy(j).start())

    def middle(self):
        self.each(lambda j: self.scatter_copy(j).wait_recv())
        me = self.place.hid
        total = self.parts[me].astype(F32)
        for j in range(1, self.place.nh):
            total = total + self.got[j].astype(F32)
        self.whole[me] = total.astype(BF16)
        self.each(lambda j: self.gather_copy(j, me).start())

    def end(self):
        nh = self.place.nh

        def wait(j):
            self.gather_copy(j, lax.rem(self.place.hid + nh - j, nh)).wait_recv()

        self.each(wait)

    def finish(self):
        def wait(j):
            self.scatter_copy(j).wait_send()
            self.gather_copy(j, self.place.hid).wait_send()

        self.each(wait)


def layer(
    nx, nz, nh, scale,
    x_ref, g_ref, home, bu_ref, bd_ref, ul_ref, ur_ref, dl_ref, dr_ref,
    out_ref, ig_ref, gbu_ref, gbd_ref, gul_ref, gur_ref, gdl_ref, gdr_ref,
    g_low, g_all, t_low, t_all,
    low_first, low_second, all_z1, all_x2, all_x1, all_z2,
    w_up, w_down, m_one, m_two, xs, gs, xt, hid_t, gp, hid_m, gp_m,
    rank_parts, rank_got, rank_one, rank_two,
    side_send, side_mid, side_end,
    ag_send, ag_recv, rs_send, rs_recv, rank_sems, low_sems, y_sems,
):
    place = Place(nx, nz, nh)
    rows, blk = bu_ref.shape[2], bu_ref.shape[3]
    tokens = x_ref.shape[0]
    hb = bu_ref.shape[0]
    half = rows // 2
    px, pz = place.pos["x"], place.pos["z"]

    barrier = pltpu.get_barrier_semaphore()
    for axis in ("x", "z"):
        for o in range(1, place.size[axis]):
            pl.semaphore_signal(barrier, inc=1, device_id=place.neighbour(axis, o), device_id_type=MESH)

    @pl.loop(1, nh)
    def _(j):
        pl.semaphore_signal(barrier, inc=1, device_id=place.peer(j), device_id_type=MESH)

    hidden_dev, width_dev = ur_ref.shape[1], dr_ref.shape[1]
    g_low[px, pz] = jnp.concatenate([ul_ref[...].astype(F32), dr_ref[...].astype(F32)], axis=0).astype(BF16)
    downs = SLOTS * hb * blk
    ranks = 2 * downs
    g_all[px, pz, :, ranks:] = jnp.concatenate(
        [ur_ref[...].astype(F32), dl_ref[...].astype(F32)], axis=0
    ).astype(BF16)
    for s in range(SLOTS):
        for h in range(hb):
            at = (s * hb + h) * blk
            g_all[px, pz, :, at : at + blk] = bu_ref[h, s]
            g_all[px, pz, :, downs + at : downs + at + blk] = bd_ref[h, s]
    for b in range(2):
        xs[0, b] = x_ref[:, b * blk : (b + 1) * blk]
        gs[0, b] = g_ref[:, b * blk : (b + 1) * blk]
    pl.semaphore_wait(barrier, nx + nz + nh - 3)

    gathers = [TorusGather(place, g_all, kind, ag_send, ag_recv) for kind in range(2)]
    low_gather = DirectGather(place, g_low, low_sems.at[0])
    rounds = nx // 2 + nz // 2

    def gather_step(k):
        for one_half in gathers:
            one_half.advance(k)

    part = tokens // 2
    pieces = [(ref, b, q) for ref in (xs, gs) for b in range(2) for q in range(2)]

    def y_copy(i, stage):
        ref, b, q = pieces[i]
        at = pl.ds(q * part, part)
        return pltpu.make_async_remote_copy(
            src_ref=ref.at[0 if stage == 0 else 2, b, at],
            dst_ref=ref.at[2 if stage == 0 else 1, b, at],
            send_sem=y_sems.at[stage, 0, i],
            recv_sem=y_sems.at[stage, 1, i],
            device_id=place.near if stage == 0 else place.far,
            device_id_type=MESH,
        )

    def pass_on(i):
        y_copy(i, 0).wait_recv()
        y_copy(i, 1).start()

    column = lax.broadcasted_iota(jnp.int32, (tokens, blk), 1)
    is_low = lax.rem(column, rows) < half

    def flat(buf, at, width):
        return buf[:, :, :, at : at + width].astype(F32).reshape(blk, width).astype(BF16)

    one = RankSum(place, rank_parts.at[0], rank_got.at[0], rank_one, rank_sems.at[0])
    two = RankSum(place, rank_parts.at[1], rank_got.at[1], rank_two, rank_sems.at[1])

    def rank_start(which, index, low, high):
        mixed = jnp.where(is_low, low, high).reshape(nh, tokens // nh, blk)
        rank_parts[index] = mixed.astype(BF16)
        which.start()

    def exchange(begun, passed):
        for i in begun:
            y_copy(i, 0).start()
        for i in passed:
            pass_on(i)

    low_gather.begin(0)
    gather_step(0)
    exchange((0, 1), ())
    low_gather.wait(0)
    low_gather.begin(1)
    gather_step(1)
    exchange((2, 3), (0,))
    gather_step(2)
    exchange((4, 5), (1, 2))
    low_gather.wait(1)
    for j in range(2):
        m_two[:, j * blk : (j + 1) * blk] = flat(g_low, j * blk, blk)
    rank_start(one, 0, dot(x_ref[...], m_two[...], NT), dot(g_ref[...], m_two[...], NT))
    gather_step(3)
    exchange((6, 7), (3, 4))
    gather_step(4)
    exchange((), (5, 6))
    one.middle()
    gather_step(5)
    exchange((), (7,))
    for i in range(4):
        y_copy(i, 1).wait_recv()
    for s in range(SLOTS):
        for b in range(2):
            xt[s, b] = xs[s, b].T
    for k in range(6, rounds + 1):
        gather_step(k)
    for j in range(SLOTS * hb):
        w_up[j // hb, :, (j % hb) * blk : (j % hb + 1) * blk] = flat(g_all, j * blk, blk)
        w_down[j // hb, (j % hb) * blk : (j % hb + 1) * blk, :] = flat(g_all, downs + j * blk, blk)
    for j in range(hb):
        m_one[:, j * blk : (j + 1) * blk] = flat(g_all, ranks + j * blk, blk)
    for i in range(4, 8):
        y_copy(i, 1).wait_recv()
    one.end()

    rank1 = rank_one[...].reshape(tokens, blk)
    zero = jnp.zeros_like(rank1)
    rank_in = jnp.where(is_low, rank1, zero)
    rank_back = jnp.where(is_low, zero, rank1)

    @pl.loop(0, hb)
    def _(h):
        home_h = home[h]
        at = pl.ds(pl.multiple_of(h * blk, blk), blk)
        value = dot(rank_in, m_one[:, at])
        grad = dot(rank_back, m_one[:, at])
        for s in range(SLOTS):
            value = value + dot(xs[s, home_h], w_up[s, :, at])
            grad = grad + dot(gs[s, home_h], w_down[s, at, :], NT)
        activated, derivative = gelu_pair(value)
        hidden = activated.astype(BF16)
        grad_pre = (grad * derivative).astype(BF16)
        hid_t[h] = hidden.T
        gp[h] = grad_pre
        for b in range(2):
            keep = jnp.where(home_h == b, 1.0, 0.0).astype(F32)
            hid_m[b, :, at] = (hidden.astype(F32) * keep).astype(BF16)
            gp_m[b, :, at] = (grad_pre.astype(F32) * keep).astype(BF16)

    def side(tensor, s, b):
        if tensor == 0:
            return dot(hid_m[b], w_down[s])
        return dot(gp_m[b], w_up[s], NT)

    sides = [(tensor, b) for tensor in range(2) for b in range(2)]

    def side_copy(i, stage):
        tensor, b = sides[i]
        return pltpu.make_async_remote_copy(
            src_ref=(side_send if stage == 0 else side_mid).at[tensor, b],
            dst_ref=(side_mid if stage == 0 else side_end).at[tensor, b],
            send_sem=y_sems.at[2 + stage, 0, i],
            recv_sem=y_sems.at[2 + stage, 1, i],
            device_id=place.far if stage == 0 else place.near,
            device_id_type=MESH,
        )

    hidden_all = hid_m[0] + hid_m[1]
    grad_all = gp_m[0] + gp_m[1]
    rank_start(
        two, 1, dot(grad_all, m_one[...], NT), dot(hidden_all, m_one[...], NT)
    )

    def side_begin(i):
        tensor, b = sides[i]
        side_send[tensor, b] = side(tensor, 1, b).astype(BF16)
        side_copy(i, 0).start()

    for i in range(2):
        side_begin(i)

    scatters = [
        Scatter(
            place, t_all, kind, scatter_widths(t_all.shape[3]),
            *((all_z1, all_x2) if kind < 2 else (all_x1, all_z2)),
            rs_send, rs_recv,
        )
        for kind in range(4)
    ]
    low_scatter = DirectScatter(place, t_low, low_first, low_second, low_sems.at[1])

    def scatter_step(k):
        for one_chunk in scatters:
            one_chunk.advance(k)

    def shaped(value):
        return (value * scale).reshape(nx, nz, rows, value.shape[1]).astype(BF16)

    @pl.loop(0, hb)
    def _(h):
        home_h = home[h]
        for s in range(SLOTS):
            at = pl.ds(pl.multiple_of((s * hb + h) * blk, blk), blk)
            t_all[:, :, :, at] = shaped(dot(xt[s, home_h], gp[h]))
            at = pl.ds(pl.multiple_of(downs + (s * hb + h) * blk, blk), blk)
            t_all[:, :, :, at] = shaped(dot(hid_t[h], gs[s, home_h]))

    rank_in_t = rank_in.T
    rank_back_t = rank_back.T
    for j in range(hb):
        at = slice(j * blk, (j + 1) * blk)
        t_all[:, :, :, ranks + j * blk : ranks + (j + 1) * blk] = shaped(
            dot(rank_in_t, grad_all[:, at]) + dot(rank_back_t, hidden_all[:, at])
        )
    scatter_step(0)

    def side_pass(i):
        tensor, b = sides[i]
        own = side(tensor, 2, b)
        side_copy(i, 0).wait_recv()
        side_mid[tensor, b] = (side_mid[tensor, b].astype(F32) + own).astype(BF16)
        side_copy(i, 1).start()

    scatter_step(1)
    side_begin(2)
    two.middle()
    side_pass(0)
    scatter_step(2)
    side_begin(3)
    side_pass(1)
    two.end()
    rank2 = rank_two[...].reshape(tokens, blk)
    rank_grad = jnp.where(is_low, rank2, zero)
    rank_mid = jnp.where(is_low, zero, rank2)
    rank_grad_t = rank_grad.T
    rank_mid_t = rank_mid.T
    for j in range(2):
        at = slice(j * blk, (j + 1) * blk)
        t_low[:, :, :, at] = shaped(dot(rank_grad_t, x_ref[:, at]) + dot(rank_mid_t, g_ref[:, at]))
    low_scatter.begin(0)

    def result(i):
        tensor, b = sides[i]
        at = slice(b * blk, (b + 1) * blk)
        rank = rank_mid if tensor == 0 else rank_grad
        total = side(tensor, 0, b) + dot(rank, m_two[:, at])
        side_copy(i, 1).wait_recv()
        total = total + side_end[tensor, b].astype(F32)
        ref = out_ref if tensor == 0 else ig_ref
        ref[:, at] = total.astype(BF16)

    scatter_step(3)
    side_pass(2)
    scatter_step(4)
    low_scatter.wait(0)
    low_scatter.begin(1)
    side_pass(3)
    result(0)
    result(1)
    scatter_step(5)
    low_scatter.wait(1)
    low = low_scatter.result
    gul_ref[...] = low[:half].astype(BF16)
    gdr_ref[...] = low[half:].astype(BF16)
    result(2)
    for k in range(6, rounds + 1):
        scatter_step(k)
    result(3)

    total = jnp.concatenate([one_chunk.result for one_chunk in scatters], axis=1)
    for first, ref in ((0, gbu_ref), (downs, gbd_ref)):
        for s in range(SLOTS):
            for h in range(hb):
                at = first + (s * hb + h) * blk
                ref[h, s] = total[:, at : at + blk].astype(BF16)
    gur_ref[...] = total[:half, ranks:].astype(BF16)
    gdl_ref[...] = total[half:, ranks:].astype(BF16)

    for one_chunk in gathers + scatters + [low_gather, low_scatter]:
        one_chunk.finish()
    for i in range(8):
        y_copy(i, 0).wait_send()
        y_copy(i, 1).wait_send()
    for i in range(4):
        side_copy(i, 0).wait_send()
        side_copy(i, 1).wait_send()
    one.finish()
    two.finish()


def hand_over(*refs):
    n = len(refs) // 2
    for source, target in zip(refs[:n], refs[n:]):
        target[...] = source[...]


def per_device(
    nx, nz, nh,
    inputs, out_grad, home_block, blocks_up, blocks_down, up_left, up_right, down_left, down_right,
):
    tokens, width_dev = inputs.shape
    hb, slots, rows, blk = blocks_up.shape
    hidden_dev = hb * blk
    scale = float(nx * nz * tokens) ** (-0.5)
    all_cols = 2 * slots * hb * blk + hidden_dev
    vmem = pl.BlockSpec(memory_space=pltpu.VMEM)
    smem = pl.BlockSpec(memory_space=pltpu.SMEM)

    def buf(shape, dtype=BF16):
        return pltpu.VMEM(shape, dtype)

    gathered = [buf((nx, nz, rows, c)) for c in (width_dev, all_cols)]
    w_z, w_x = scatter_widths(all_cols)[0], scatter_widths(all_cols)[3]
    landing = [
        buf((nz, nx, rows, width_dev)),
        buf((nx, rows, width_dev)),
        buf((2, nz - 1, nx, rows, w_z)),
        buf((2, nx - 1, rows, w_z)),
        buf((2, nx - 1, nz, rows, w_x)),
        buf((2, nz - 1, rows, w_x)),
    ]
    ups = up_left.T, down_left.T
    outs = pl.pallas_call(
        functools.partial(layer, nx, nz, nh, scale),
        out_shape=[
            jax.ShapeDtypeStruct(a.shape, BF16)
            for a in (
                inputs, out_grad, blocks_up, blocks_down, ups[0], up_right, ups[1], down_right,
            )
        ],
        in_specs=[vmem, vmem, smem] + [vmem] * 6,
        out_specs=[vmem] * 8,
        scratch_shapes=gathered
        + gathered
        + landing
        + [
            buf((slots, blk, hidden_dev)),
            buf((slots, hidden_dev, blk)),
            buf((blk, hidden_dev)),
            buf((blk, width_dev)),
            buf((slots, 2, tokens, blk)),
            buf((slots, 2, tokens, blk)),
            buf((slots, 2, blk, tokens)),
            buf((hb, blk, tokens)),
            buf((hb, tokens, blk)),
            buf((2, tokens, hidden_dev)),
            buf((2, tokens, hidden_dev)),
            buf((2, nh, tokens // nh, blk)),
            buf((2, nh, tokens // nh, blk)),
            buf((nh, tokens // nh, blk)),
            buf((nh, tokens // nh, blk)),
            buf((2, 2, tokens, blk)),
            buf((2, 2, tokens, blk)),
            buf((2, 2, tokens, blk)),
            pltpu.SemaphoreType.DMA((2, max(nx, nz) * (min(nx, nz) + 1))),
            pltpu.SemaphoreType.DMA((2, max(nx, nz) * (min(nx, nz) + 1))),
            pltpu.SemaphoreType.DMA((4, 4)),
            pltpu.SemaphoreType.DMA((4, nx + nz - 2)),
            pltpu.SemaphoreType.DMA((2, 4, nh)),
            pltpu.SemaphoreType.DMA((2, 2, 2, max(nx, nz))),
            pltpu.SemaphoreType.DMA((4, 2, 8)),
        ],
        compiler_params=pltpu.CompilerParams(
            collective_id=0, has_side_effects=True, vmem_limit_bytes=60 * 2**20
        ),
    )(
        inputs, out_grad, home_block, blocks_up, blocks_down, ups[0], up_right, ups[1], down_right,
    )
    out, ig, gbu, gbd, gul, gur, gdl, gdr = pl.pallas_call(
        hand_over,
        out_shape=[jax.ShapeDtypeStruct(a.shape, a.dtype) for a in outs],
        in_specs=[vmem] * len(outs),
        out_specs=[vmem] * len(outs),
    )(*outs)
    return out, ig, gbu, gbd, gul.T, gur, gdl.T, gdr


def solution(mesh, nx=4):
    n_dp, nh = mesh.shape["dp"], mesh.shape["hid"]
    placed = (
        P("dp", "hid"),
        P("dp", "hid"),
        P("hid"),
        P("hid", None, "dp", None),
        P("hid", None, "dp", None),
        P("hid", "dp"),
        P("dp", "hid"),
        P("hid", "dp"),
        P("dp", "hid"),
    )
    return jax.shard_map(
        functools.partial(per_device, nx, n_dp // nx, nh),
        mesh=mesh,
        in_specs=placed,
        out_specs=(
            P("dp", "hid"),
            P("dp", "hid"),
            P("hid", None, "dp", None),
            P("hid", None, "dp", None),
            P("hid", "dp"),
            P("dp", "hid"),
            P("hid", "dp"),
            P("dp", "hid"),
        ),
        check_vma=False,
    )
```

```python
import functools

import jax
import jax.numpy as jnp
from jax import lax
from jax.experimental import pallas as pl
from jax.experimental.pallas import tpu as pltpu
from jax.sharding import PartitionSpec as P

MESH = pl.DeviceIdType.MESH
gelu_coef = 0.7978845608028654
cubic_coef = 0.044715
SLOTS = 3
F32 = jnp.float32
BF16 = jnp.bfloat16
NN = (((1,), (0,)), ((), ()))
NT = (((1,), (1,)), ((), ()))


def dot(a, b, dims=NN):
    return lax.dot_general(a, b, dims, preferred_element_type=F32)


def flip(index, bit):
    return index + bit - 2 * bit * lax.rem(lax.div(index, bit), 2)


def wrap(value, n):
    return lax.rem(value + 4 * n, n)


def gelu_pair(pre_act):
    tangent = jnp.tanh(gelu_coef * (pre_act + cubic_coef * pre_act * pre_act * pre_act))
    activated = 0.5 * pre_act * (1.0 + tangent)
    derivative = 0.5 * (1.0 + tangent) + 0.5 * pre_act * (1.0 - tangent * tangent) * gelu_coef * (
        1.0 + 3.0 * cubic_coef * pre_act * pre_act
    )
    return activated, derivative


class Place:
    def __init__(self, nx, nz, nh):
        self.size = {"x": nx, "z": nz}
        self.nh = nh
        self.dp = lax.axis_index("dp")
        self.hid = lax.axis_index("hid")
        self.pos = {"x": lax.div(self.dp, nz), "z": lax.rem(self.dp, nz)}
        self.near = (self.dp, flip(self.hid, nh // 4))
        self.far = (self.dp, flip(flip(self.hid, nh // 4), nh // 2))

    def neighbour(self, axis, o):
        x, z = self.pos["x"], self.pos["z"]
        if axis == "x":
            x = wrap(x + o, self.size["x"])
        else:
            z = wrap(z + o, self.size["z"])
        return (x * self.size["z"] + z, self.hid)

    def peer(self, j):
        return (self.dp, lax.rem(self.hid + j, self.nh))


def gather_axes(kind):
    return ("x", "z") if kind < 2 else ("z", "x")


def ring_dirs(n):
    return [(0, n // 2)] + ([(1, n // 2 - 1)] if n > 2 else [])


def scatter_widths(total):
    return [11 * total // 56] * 2 + [17 * total // 56] * 2


class TorusGather:
    def __init__(self, place, buf, kind, send_sem, recv_sem):
        self.place, self.buf, self.kind = place, buf, kind
        total = buf.shape[3]
        self.first, self.width = ((0, 11 * total // 28), (11 * total // 28, 17 * total // 28))[kind]
        self.axes = ("x", "z") if kind == 0 else ("z", "x")
        self.n = [place.size[a] for a in self.axes]
        self.send_sem, self.recv_sem = send_sem, recv_sem
        self.rounds = self.n[0] // 2 + self.n[1] // 2
        self.sent = []
        self.count = 0
        self.ids = {}

    def view(self, f, g, part):
        at = {}
        for axis, n, off in zip(self.axes, self.n, (f, g)):
            at[axis] = wrap(self.place.pos[axis] - off, n)
        first, width = self.first, self.width
        if part is not None:
            width = width // 2
            first = first + part * width
        return self.buf.at[at["x"], at["z"], :, pl.ds(first, width)]

    def copy(self, level, f, g, o, ref):
        at = self.ids.setdefault((level, f, g, o), len(self.ids))
        return pltpu.make_async_remote_copy(
            src_ref=ref,
            dst_ref=ref,
            send_sem=self.send_sem.at[self.kind, at],
            recv_sem=self.recv_sem.at[self.kind, at],
            device_id=self.place.neighbour(self.axes[level], o),
            device_id_type=MESH,
        )

    def send(self, level, f, g, o, part):
        made = self.copy(level, f, g, o, self.view(f, g, part))
        made.start()
        self.sent.append(made)

    def spread(self, level, f, g):
        here = f if level == 0 else g
        half = self.n[level] // 2
        for o in (1, -1):
            if here * o < 0 or abs(here) >= half:
                continue
            part = None if abs(here) + 1 < half else (0 if o > 0 else 1)
            self.send(level, f, g, o, part)

    def stops(self, level):
        half = self.n[level] // 2
        return [(0, 0)] + [(o * t, t) for t in range(1, half) for o in (1, -1)] + [(half, half)]

    def arrive(self, level, f, g):
        here = f if level == 0 else g
        half = self.n[level] // 2
        for o in (1, -1):
            if here * o < 0 and abs(here) < half:
                continue
            last = o * (abs(here) - 1)
            back = (last, g) if level == 0 else (f, last)
            part = None if abs(here) < half else (0 if o > 0 else 1)
            self.copy(level, *back, o, self.view(f, g, part)).wait_recv()

    def advance(self, k):
        for f, a in self.stops(0):
            if a == k:
                if a:
                    self.arrive(0, f, 0)
                self.spread(0, f, 0)
                self.spread(1, f, 0)
        for f, a in self.stops(0):
            for g, b in self.stops(1):
                if b and a + b == k:
                    self.arrive(1, f, g)
                    self.spread(1, f, g)

    def finish(self):
        for made in self.sent:
            made.wait_send()
        self.sent = []


class Scatter:
    def __init__(self, place, terms, kind, widths, first_buf, second_buf, send_sem, recv_sem):
        self.place, self.terms, self.kind = place, terms, kind
        first = sum(widths[:kind])
        self.columns = pl.ds(first, widths[kind])
        self.bufs = (first_buf, second_buf)
        self.send_sem, self.recv_sem = send_sem, recv_sem
        self.axes = gather_axes(kind)[::-1]
        self.turns = [place.size[a] // 2 for a in self.axes]
        self.rounds = sum(self.turns)
        self.sent = {}

    def term(self, phase, at):
        axis = self.axes[phase]
        own = self.place.pos
        if phase == 1:
            x, z = (at, own["z"]) if axis == "x" else (own["x"], at)
            return self.terms.at[x, z, :, self.columns]
        if axis == "x":
            return self.terms.at[at, :, :, self.columns]
        return self.terms.at[:, at, :, self.columns]

    def slot(self, phase, d, t):
        n = self.place.size[self.axes[phase]]
        return (n // 2 if d else 0) + t - 1

    def arrived(self, phase, d, t):
        return self.bufs[phase].at[self.kind % 2, self.slot(phase, d, t)]

    def o(self, d):
        return (1 if self.kind % 2 == 0 else -1) * (1 if d == 0 else -1)

    def copy(self, phase, d, t, source):
        axis = self.axes[phase]
        first = 0 if phase == 0 else self.place.size[self.axes[0]] - 1
        return pltpu.make_async_remote_copy(
            src_ref=source,
            dst_ref=self.arrived(phase, d, t),
            send_sem=self.send_sem.at[self.kind, phase * 2 + d],
            recv_sem=self.recv_sem.at[self.kind, first + self.slot(phase, d, t)],
            device_id=self.place.neighbour(axis, self.o(d)),
            device_id_type=MESH,
        )

    def send(self, phase, d, t, source):
        before = self.sent.pop((phase, d), None)
        if before is not None:
            before.wait_send()
        made = self.copy(phase, d, t, source)
        made.start()
        self.sent[(phase, d)] = made

    def dest(self, phase, d, t, count):
        axis = self.axes[phase]
        return wrap(self.place.pos[axis] + self.o(d) * (count - t + 1), self.place.size[axis])

    def begin(self, phase):
        for d, count in ring_dirs(self.place.size[self.axes[phase]]):
            self.send(phase, d, 1, self.term(phase, self.dest(phase, d, 1, count)))

    def advance(self, k):
        if k == 0:
            self.begin(0)
            return
        phase = 0 if k <= self.turns[0] else 1
        t = k - (self.turns[0] if phase else 0)
        axis = self.axes[phase]
        dirs = ring_dirs(self.place.size[axis])
        for d, count in dirs:
            if t <= count:
                held = self.arrived(phase, d, t)
                self.copy(phase, d, t, held).wait_recv()
                if t < count:
                    held[...] = held[...] + self.term(phase, self.dest(phase, d, t + 1, count))[...]
                    self.send(phase, d, t + 1, held)
        if t == self.turns[phase]:
            own = self.term(phase, self.place.pos[axis])
            total = own[...].astype(F32)
            for d, count in dirs:
                total = total + self.arrived(phase, d, count)[...].astype(F32)
            if phase == 0:
                own[...] = total.astype(BF16)
                self.begin(1)
            else:
                self.result = total

    def finish(self):
        for made in self.sent.values():
            made.wait_send()
        self.sent = {}


class DirectGather:
    def __init__(self, place, buf, sems):
        self.place, self.buf, self.sems = place, buf, sems

    def copies(self, phase, sending):
        place = self.place
        axis = "xz"[phase]
        n = place.size[axis]
        made = []
        for j in range(1, n):
            if phase == 0:
                at = place.pos["x"] if sending else wrap(place.pos["x"] - j, n)
                ref = self.buf.at[at, place.pos["z"]]
            else:
                at = place.pos["z"] if sending else wrap(place.pos["z"] - j, n)
                ref = self.buf.at[:, at]
            made.append(
                pltpu.make_async_remote_copy(
                    src_ref=ref,
                    dst_ref=ref,
                    send_sem=self.sems.at[0, phase, j],
                    recv_sem=self.sems.at[1, phase, j],
                    device_id=place.neighbour(axis, j),
                    device_id_type=MESH,
                )
            )
        return made

    def begin(self, phase):
        for made in self.copies(phase, True):
            made.start()

    def wait(self, phase):
        for made in self.copies(phase, False):
            made.wait_recv()

    def finish(self):
        for phase in range(2):
            for made in self.copies(phase, True):
                made.wait_send()


class DirectScatter:
    def __init__(self, place, terms, first_buf, second_buf, sems):
        self.place, self.terms, self.sems = place, terms, sems
        self.bufs = (first_buf, second_buf)

    def term(self, phase, at):
        if phase == 0:
            return self.terms.at[:, at]
        return self.terms.at[at, self.place.pos["z"]]

    def copies(self, phase):
        place = self.place
        axis = "zx"[phase]
        n = place.size[axis]
        return [
            pltpu.make_async_remote_copy(
                src_ref=self.term(phase, wrap(place.pos[axis] + j, n)),
                dst_ref=self.bufs[phase].at[j],
                send_sem=self.sems.at[0, phase, j],
                recv_sem=self.sems.at[1, phase, j],
                device_id=place.neighbour(axis, j),
                device_id_type=MESH,
            )
            for j in range(1, n)
        ]

    def begin(self, phase):
        for made in self.copies(phase):
            made.start()

    def wait(self, phase):
        axis = "zx"[phase]
        for made in self.copies(phase):
            made.wait_recv()
        own = self.term(phase, self.place.pos[axis])
        total = own[...].astype(F32)
        for j in range(1, self.place.size[axis]):
            total = total + self.bufs[phase][j].astype(F32)
        if phase == 0:
            own[...] = total.astype(BF16)
        else:
            self.result = total

    def finish(self):
        for phase in range(2):
            for made in self.copies(phase):
                made.wait_send()


class RankSum:
    def __init__(self, place, parts, arrived, whole, sems):
        self.place, self.parts, self.got, self.whole, self.sems = place, parts, arrived, whole, sems

    def scatter_copy(self, j):
        peer = self.place.peer(j)
        return pltpu.make_async_remote_copy(
            src_ref=self.parts.at[peer[1]],
            dst_ref=self.got.at[j],
            send_sem=self.sems.at[0, j],
            recv_sem=self.sems.at[1, j],
            device_id=peer,
            device_id_type=MESH,
        )

    def gather_copy(self, j, at):
        return pltpu.make_async_remote_copy(
            src_ref=self.whole.at[at],
            dst_ref=self.whole.at[at],
            send_sem=self.sems.at[2, j],
            recv_sem=self.sems.at[3, j],
            device_id=self.place.peer(j),
            device_id_type=MESH,
        )

    def each(self, body):
        @pl.loop(1, self.place.nh)
        def _(j):
            body(j)

    def start(self):
        self.each(lambda j: self.scatter_copy(j).start())

    def middle(self):
        self.each(lambda j: self.scatter_copy(j).wait_recv())
        me = self.place.hid
        total = self.parts[me].astype(F32)
        for j in range(1, self.place.nh):
            total = total + self.got[j].astype(F32)
        self.whole[me] = total.astype(BF16)
        self.each(lambda j: self.gather_copy(j, me).start())

    def end(self):
        nh = self.place.nh

        def wait(j):
            self.gather_copy(j, lax.rem(self.place.hid + nh - j, nh)).wait_recv()

        self.each(wait)

    def finish(self):
        def wait(j):
            self.scatter_copy(j).wait_send()
            self.gather_copy(j, self.place.hid).wait_send()

        self.each(wait)


def layer(
    nx, nz, nh, scale,
    x_ref, g_ref, home, bu_ref, bd_ref, ul_ref, ur_ref, dl_ref, dr_ref,
    out_ref, ig_ref, gbu_ref, gbd_ref, gul_ref, gur_ref, gdl_ref, gdr_ref,
    g_low, g_all, t_low, t_all,
    low_first, low_second, all_z1, all_x2, all_x1, all_z2,
    w_up, w_down, m_one, m_two, xs, gs, xt, hid_t, gp, hid_m, gp_m,
    rank_parts, rank_got, rank_one, rank_two,
    side_send, side_mid, side_end,
    ag_send, ag_recv, rs_send, rs_recv, rank_sems, low_sems, y_sems,
):
    place = Place(nx, nz, nh)
    rows, blk = bu_ref.shape[2], bu_ref.shape[3]
    tokens = x_ref.shape[0]
    hb = bu_ref.shape[0]
    half = rows // 2
    px, pz = place.pos["x"], place.pos["z"]

    barrier = pltpu.get_barrier_semaphore()
    for axis in ("x", "z"):
        for o in range(1, place.size[axis]):
            pl.semaphore_signal(barrier, inc=1, device_id=place.neighbour(axis, o), device_id_type=MESH)

    @pl.loop(1, nh)
    def _(j):
        pl.semaphore_signal(barrier, inc=1, device_id=place.peer(j), device_id_type=MESH)

    hidden_dev, width_dev = ur_ref.shape[1], dr_ref.shape[1]
    g_low[px, pz] = jnp.concatenate([ul_ref[...].astype(F32), dr_ref[...].astype(F32)], axis=0).astype(BF16)
    downs = SLOTS * hb * blk
    ranks = 2 * downs
    g_all[px, pz, :, ranks:] = jnp.concatenate(
        [ur_ref[...].astype(F32), dl_ref[...].astype(F32)], axis=0
    ).astype(BF16)
    for s in range(SLOTS):
        for h in range(hb):
            at = (s * hb + h) * blk
            g_all[px, pz, :, at : at + blk] = bu_ref[h, s]
            g_all[px, pz, :, downs + at : downs + at + blk] = bd_ref[h, s]
    for b in range(2):
        xs[0, b] = x_ref[:, b * blk : (b + 1) * blk]
        gs[0, b] = g_ref[:, b * blk : (b + 1) * blk]
    pl.semaphore_wait(barrier, nx + nz + nh - 3)

    gathers = [TorusGather(place, g_all, kind, ag_send, ag_recv) for kind in range(2)]
    low_gather = DirectGather(place, g_low, low_sems.at[0])
    rounds = nx // 2 + nz // 2

    def gather_step(k):
        for one_half in gathers:
            one_half.advance(k)

    part = tokens // 2
    pieces = [(ref, b, q) for ref in (xs, gs) for b in range(2) for q in range(2)]

    def y_copy(i, stage):
        ref, b, q = pieces[i]
        at = pl.ds(q * part, part)
        return pltpu.make_async_remote_copy(
            src_ref=ref.at[0 if stage == 0 else 2, b, at],
            dst_ref=ref.at[2 if stage == 0 else 1, b, at],
            send_sem=y_sems.at[stage, 0, i],
            recv_sem=y_sems.at[stage, 1, i],
            device_id=place.near if stage == 0 else place.far,
            device_id_type=MESH,
        )

    def pass_on(i):
        y_copy(i, 0).wait_recv()
        y_copy(i, 1).start()

    column = lax.broadcasted_iota(jnp.int32, (tokens, blk), 1)
    is_low = lax.rem(column, rows) < half

    def flat(buf, at, width):
        return buf[:, :, :, at : at + width].astype(F32).reshape(blk, width).astype(BF16)

    one = RankSum(place, rank_parts.at[0], rank_got.at[0], rank_one, rank_sems.at[0])
    two = RankSum(place, rank_parts.at[1], rank_got.at[1], rank_two, rank_sems.at[1])

    def rank_start(which, index, low, high):
        mixed = jnp.where(is_low, low, high).reshape(nh, tokens // nh, blk)
        rank_parts[index] = mixed.astype(BF16)
        which.start()

    def exchange(begun, passed):
        for i in begun:
            y_copy(i, 0).start()
        for i in passed:
            pass_on(i)

    low_gather.begin(0)
    gather_step(0)
    exchange((0, 1), ())
    low_gather.wait(0)
    low_gather.begin(1)
    gather_step(1)
    exchange((2, 3), (0,))
    gather_step(2)
    exchange((4, 5), (1, 2))
    low_gather.wait(1)
    for j in range(2):
        m_two[:, j * blk : (j + 1) * blk] = flat(g_low, j * blk, blk)
    rank_start(one, 0, dot(x_ref[...], m_two[...], NT), dot(g_ref[...], m_two[...], NT))
    gather_step(3)
    exchange((6, 7), (3, 4))
    gather_step(4)
    exchange((), (5, 6))
    one.middle()
    gather_step(5)
    exchange((), (7,))
    for i in range(4):
        y_copy(i, 1).wait_recv()
    for s in range(SLOTS):
        for b in range(2):
            xt[s, b] = xs[s, b].T
    for k in range(6, rounds + 1):
        gather_step(k)
    for j in range(SLOTS * hb):
        w_up[j // hb, :, (j % hb) * blk : (j % hb + 1) * blk] = flat(g_all, j * blk, blk)
        w_down[j // hb, (j % hb) * blk : (j % hb + 1) * blk, :] = flat(g_all, downs + j * blk, blk)
    for j in range(hb):
        m_one[:, j * blk : (j + 1) * blk] = flat(g_all, ranks + j * blk, blk)
    for i in range(4, 8):
        y_copy(i, 1).wait_recv()
    one.end()

    rank1 = rank_one[...].reshape(tokens, blk)
    zero = jnp.zeros_like(rank1)
    rank_in = jnp.where(is_low, rank1, zero)
    rank_back = jnp.where(is_low, zero, rank1)

    @pl.loop(0, hb)
    def _(h):
        home_h = home[h]
        at = pl.ds(pl.multiple_of(h * blk, blk), blk)
        value = dot(rank_in, m_one[:, at])
        grad = dot(rank_back, m_one[:, at])
        for s in range(SLOTS):
            value = value + dot(xs[s, home_h], w_up[s, :, at])
            grad = grad + dot(gs[s, home_h], w_down[s, at, :], NT)
        activated, derivative = gelu_pair(value)
        hidden = activated.astype(BF16)
        grad_pre = (grad * derivative).astype(BF16)
        hid_t[h] = hidden.T
        gp[h] = grad_pre
        for b in range(2):
            keep = jnp.where(home_h == b, 1.0, 0.0).astype(F32)
            hid_m[b, :, at] = (hidden.astype(F32) * keep).astype(BF16)
            gp_m[b, :, at] = (grad_pre.astype(F32) * keep).astype(BF16)

    def side(tensor, s, b):
        if tensor == 0:
            return dot(hid_m[b], w_down[s])
        return dot(gp_m[b], w_up[s], NT)

    sides = [(tensor, b) for tensor in range(2) for b in range(2)]

    def side_copy(i, stage):
        tensor, b = sides[i]
        return pltpu.make_async_remote_copy(
            src_ref=(side_send if stage == 0 else side_mid).at[tensor, b],
            dst_ref=(side_mid if stage == 0 else side_end).at[tensor, b],
            send_sem=y_sems.at[2 + stage, 0, i],
            recv_sem=y_sems.at[2 + stage, 1, i],
            device_id=place.far if stage == 0 else place.near,
            device_id_type=MESH,
        )

    hidden_all = hid_m[0] + hid_m[1]
    grad_all = gp_m[0] + gp_m[1]
    rank_start(
        two, 1, dot(grad_all, m_one[...], NT), dot(hidden_all, m_one[...], NT)
    )

    def side_begin(i):
        tensor, b = sides[i]
        side_send[tensor, b] = side(tensor, 1, b).astype(BF16)
        side_copy(i, 0).start()

    for i in range(2):
        side_begin(i)

    scatters = [
        Scatter(
            place, t_all, kind, scatter_widths(t_all.shape[3]),
            *((all_z1, all_x2) if kind < 2 else (all_x1, all_z2)),
            rs_send, rs_recv,
        )
        for kind in range(4)
    ]
    low_scatter = DirectScatter(place, t_low, low_first, low_second, low_sems.at[1])

    def scatter_step(k):
        for one_chunk in scatters:
            one_chunk.advance(k)

    def shaped(value):
        return (value * scale).reshape(nx, nz, rows, value.shape[1]).astype(BF16)

    @pl.loop(0, hb)
    def _(h):
        home_h = home[h]
        for s in range(SLOTS):
            at = pl.ds(pl.multiple_of((s * hb + h) * blk, blk), blk)
            t_all[:, :, :, at] = shaped(dot(xt[s, home_h], gp[h]))
            at = pl.ds(pl.multiple_of(downs + (s * hb + h) * blk, blk), blk)
            t_all[:, :, :, at] = shaped(dot(hid_t[h], gs[s, home_h]))

    rank_in_t = rank_in.T
    rank_back_t = rank_back.T
    for j in range(hb):
        at = slice(j * blk, (j + 1) * blk)
        t_all[:, :, :, ranks + j * blk : ranks + (j + 1) * blk] = shaped(
            dot(rank_in_t, grad_all[:, at]) + dot(rank_back_t, hidden_all[:, at])
        )
    scatter_step(0)

    def side_pass(i):
        tensor, b = sides[i]
        own = side(tensor, 2, b)
        side_copy(i, 0).wait_recv()
        side_mid[tensor, b] = (side_mid[tensor, b].astype(F32) + own).astype(BF16)
        side_copy(i, 1).start()

    scatter_step(1)
    side_begin(2)
    side_pass(0)
    two.middle()
    scatter_step(2)
    side_begin(3)
    side_pass(1)
    scatter_step(3)
    two.end()
    rank2 = rank_two[...].reshape(tokens, blk)
    rank_grad = jnp.where(is_low, rank2, zero)
    rank_mid = jnp.where(is_low, zero, rank2)
    rank_grad_t = rank_grad.T
    rank_mid_t = rank_mid.T
    for j in range(2):
        at = slice(j * blk, (j + 1) * blk)
        t_low[:, :, :, at] = shaped(dot(rank_grad_t, x_ref[:, at]) + dot(rank_mid_t, g_ref[:, at]))
    low_scatter.begin(0)

    def result(i):
        tensor, b = sides[i]
        at = slice(b * blk, (b + 1) * blk)
        rank = rank_mid if tensor == 0 else rank_grad
        total = side(tensor, 0, b) + dot(rank, m_two[:, at])
        side_copy(i, 1).wait_recv()
        total = total + side_end[tensor, b].astype(F32)
        ref = out_ref if tensor == 0 else ig_ref
        ref[:, at] = total.astype(BF16)

    side_pass(2)
    scatter_step(4)
    side_pass(3)
    low_scatter.wait(0)
    low_scatter.begin(1)
    result(0)
    result(1)
    scatter_step(5)
    result(2)
    for k in range(6, rounds + 1):
        scatter_step(k)
    low_scatter.wait(1)
    low = low_scatter.result
    gul_ref[...] = low[:half].astype(BF16)
    gdr_ref[...] = low[half:].astype(BF16)
    result(3)

    total = jnp.concatenate([one_chunk.result for one_chunk in scatters], axis=1)
    for first, ref in ((0, gbu_ref), (downs, gbd_ref)):
        for s in range(SLOTS):
            for h in range(hb):
                at = first + (s * hb + h) * blk
                ref[h, s] = total[:, at : at + blk].astype(BF16)
    gur_ref[...] = total[:half, ranks:].astype(BF16)
    gdl_ref[...] = total[half:, ranks:].astype(BF16)

    for one_chunk in gathers + scatters + [low_gather, low_scatter]:
        one_chunk.finish()
    for i in range(8):
        y_copy(i, 0).wait_send()
        y_copy(i, 1).wait_send()
    for i in range(4):
        side_copy(i, 0).wait_send()
        side_copy(i, 1).wait_send()
    one.finish()
    two.finish()


def hand_over(*refs):
    n = len(refs) // 2
    for source, target in zip(refs[:n], refs[n:]):
        target[...] = source[...]


def per_device(
    nx, nz, nh,
    inputs, out_grad, home_block, blocks_up, blocks_down, up_left, up_right, down_left, down_right,
):
    tokens, width_dev = inputs.shape
    hb, slots, rows, blk = blocks_up.shape
    hidden_dev = hb * blk
    scale = float(nx * nz * tokens) ** (-0.5)
    all_cols = 2 * slots * hb * blk + hidden_dev
    vmem = pl.BlockSpec(memory_space=pltpu.VMEM)
    smem = pl.BlockSpec(memory_space=pltpu.SMEM)

    def buf(shape, dtype=BF16):
        return pltpu.VMEM(shape, dtype)

    gathered = [buf((nx, nz, rows, c)) for c in (width_dev, all_cols)]
    w_z, w_x = scatter_widths(all_cols)[0], scatter_widths(all_cols)[3]
    landing = [
        buf((nz, nx, rows, width_dev)),
        buf((nx, rows, width_dev)),
        buf((2, nz - 1, nx, rows, w_z)),
        buf((2, nx - 1, rows, w_z)),
        buf((2, nx - 1, nz, rows, w_x)),
        buf((2, nz - 1, rows, w_x)),
    ]
    ups = up_left.T, down_left.T
    outs = pl.pallas_call(
        functools.partial(layer, nx, nz, nh, scale),
        out_shape=[
            jax.ShapeDtypeStruct(a.shape, BF16)
            for a in (
                inputs, out_grad, blocks_up, blocks_down, ups[0], up_right, ups[1], down_right,
            )
        ],
        in_specs=[vmem, vmem, smem] + [vmem] * 6,
        out_specs=[vmem] * 8,
        scratch_shapes=gathered
        + gathered
        + landing
        + [
            buf((slots, blk, hidden_dev)),
            buf((slots, hidden_dev, blk)),
            buf((blk, hidden_dev)),
            buf((blk, width_dev)),
            buf((slots, 2, tokens, blk)),
            buf((slots, 2, tokens, blk)),
            buf((slots, 2, blk, tokens)),
            buf((hb, blk, tokens)),
            buf((hb, tokens, blk)),
            buf((2, tokens, hidden_dev)),
            buf((2, tokens, hidden_dev)),
            buf((2, nh, tokens // nh, blk)),
            buf((2, nh, tokens // nh, blk)),
            buf((nh, tokens // nh, blk)),
            buf((nh, tokens // nh, blk)),
            buf((2, 2, tokens, blk)),
            buf((2, 2, tokens, blk)),
            buf((2, 2, tokens, blk)),
            pltpu.SemaphoreType.DMA((2, max(nx, nz) * (min(nx, nz) + 1))),
            pltpu.SemaphoreType.DMA((2, max(nx, nz) * (min(nx, nz) + 1))),
            pltpu.SemaphoreType.DMA((4, 4)),
            pltpu.SemaphoreType.DMA((4, nx + nz - 2)),
            pltpu.SemaphoreType.DMA((2, 4, nh)),
            pltpu.SemaphoreType.DMA((2, 2, 2, max(nx, nz))),
            pltpu.SemaphoreType.DMA((4, 2, 8)),
        ],
        compiler_params=pltpu.CompilerParams(
            collective_id=0, has_side_effects=True, vmem_limit_bytes=60 * 2**20
        ),
    )(
        inputs, out_grad, home_block, blocks_up, blocks_down, ups[0], up_right, ups[1], down_right,
    )
    out, ig, gbu, gbd, gul, gur, gdl, gdr = pl.pallas_call(
        hand_over,
        out_shape=[jax.ShapeDtypeStruct(a.shape, a.dtype) for a in outs],
        in_specs=[vmem] * len(outs),
        out_specs=[vmem] * len(outs),
    )(*outs)
    return out, ig, gbu, gbd, gul.T, gur, gdl.T, gdr


def solution(mesh, nx=4):
    n_dp, nh = mesh.shape["dp"], mesh.shape["hid"]
    placed = (
        P("dp", "hid"),
        P("dp", "hid"),
        P("hid"),
        P("hid", None, "dp", None),
        P("hid", None, "dp", None),
        P("hid", "dp"),
        P("dp", "hid"),
        P("hid", "dp"),
        P("dp", "hid"),
    )
    return jax.shard_map(
        functools.partial(per_device, nx, n_dp // nx, nh),
        mesh=mesh,
        in_specs=placed,
        out_specs=(
            P("dp", "hid"),
            P("dp", "hid"),
            P("hid", None, "dp", None),
            P("hid", None, "dp", None),
            P("hid", "dp"),
            P("dp", "hid"),
            P("hid", "dp"),
            P("dp", "hid"),
        ),
        check_vma=False,
    )
```

```python
import functools

import jax
import jax.numpy as jnp
from jax import lax
from jax.experimental import pallas as pl
from jax.experimental.pallas import tpu as pltpu
from jax.sharding import PartitionSpec as P

MESH = pl.DeviceIdType.MESH
gelu_coef = 0.7978845608028654
cubic_coef = 0.044715
SLOTS = 3
F32 = jnp.float32
BF16 = jnp.bfloat16
NN = (((1,), (0,)), ((), ()))
NT = (((1,), (1,)), ((), ()))


def dot(a, b, dims=NN):
    return lax.dot_general(a, b, dims, preferred_element_type=F32)


def flip(index, bit):
    return index + bit - 2 * bit * lax.rem(lax.div(index, bit), 2)


def wrap(value, n):
    return lax.rem(value + 4 * n, n)


def gelu_pair(pre_act):
    tangent = jnp.tanh(gelu_coef * (pre_act + cubic_coef * pre_act * pre_act * pre_act))
    activated = 0.5 * pre_act * (1.0 + tangent)
    derivative = 0.5 * (1.0 + tangent) + 0.5 * pre_act * (1.0 - tangent * tangent) * gelu_coef * (
        1.0 + 3.0 * cubic_coef * pre_act * pre_act
    )
    return activated, derivative


class Place:
    def __init__(self, nx, nz, nh):
        self.size = {"x": nx, "z": nz}
        self.nh = nh
        self.dp = lax.axis_index("dp")
        self.hid = lax.axis_index("hid")
        self.pos = {"x": lax.div(self.dp, nz), "z": lax.rem(self.dp, nz)}
        self.near = (self.dp, flip(self.hid, nh // 4))
        self.far = (self.dp, flip(flip(self.hid, nh // 4), nh // 2))

    def neighbour(self, axis, o):
        x, z = self.pos["x"], self.pos["z"]
        if axis == "x":
            x = wrap(x + o, self.size["x"])
        else:
            z = wrap(z + o, self.size["z"])
        return (x * self.size["z"] + z, self.hid)

    def peer(self, j):
        return (self.dp, lax.rem(self.hid + j, self.nh))


def gather_axes(kind):
    return ("x", "z") if kind < 2 else ("z", "x")


def ring_dirs(n):
    return [(0, n // 2)] + ([(1, n // 2 - 1)] if n > 2 else [])


def scatter_widths(total):
    return [11 * total // 56] * 2 + [17 * total // 56] * 2


class TorusGather:
    def __init__(self, place, buf, kind, send_sem, recv_sem):
        self.place, self.buf, self.kind = place, buf, kind
        total = buf.shape[3]
        self.first, self.width = ((0, 11 * total // 28), (11 * total // 28, 17 * total // 28))[kind]
        self.axes = ("x", "z") if kind == 0 else ("z", "x")
        self.n = [place.size[a] for a in self.axes]
        self.send_sem, self.recv_sem = send_sem, recv_sem
        self.rounds = self.n[0] // 2 + self.n[1] // 2
        self.sent = []
        self.count = 0
        self.ids = {}

    def view(self, f, g, part):
        at = {}
        for axis, n, off in zip(self.axes, self.n, (f, g)):
            at[axis] = wrap(self.place.pos[axis] - off, n)
        first, width = self.first, self.width
        if part is not None:
            width = width // 2
            first = first + part * width
        return self.buf.at[at["x"], at["z"], :, pl.ds(first, width)]

    def copy(self, level, f, g, o, ref):
        at = self.ids.setdefault((level, f, g, o), len(self.ids))
        return pltpu.make_async_remote_copy(
            src_ref=ref,
            dst_ref=ref,
            send_sem=self.send_sem.at[self.kind, at],
            recv_sem=self.recv_sem.at[self.kind, at],
            device_id=self.place.neighbour(self.axes[level], o),
            device_id_type=MESH,
        )

    def send(self, level, f, g, o, part):
        made = self.copy(level, f, g, o, self.view(f, g, part))
        made.start()
        self.sent.append(made)

    def spread(self, level, f, g):
        here = f if level == 0 else g
        half = self.n[level] // 2
        for o in (1, -1):
            if here * o < 0 or abs(here) >= half:
                continue
            part = None if abs(here) + 1 < half else (0 if o > 0 else 1)
            self.send(level, f, g, o, part)

    def stops(self, level):
        half = self.n[level] // 2
        return [(0, 0)] + [(o * t, t) for t in range(1, half) for o in (1, -1)] + [(half, half)]

    def arrive(self, level, f, g):
        here = f if level == 0 else g
        half = self.n[level] // 2
        for o in (1, -1):
            if here * o < 0 and abs(here) < half:
                continue
            last = o * (abs(here) - 1)
            back = (last, g) if level == 0 else (f, last)
            part = None if abs(here) < half else (0 if o > 0 else 1)
            self.copy(level, *back, o, self.view(f, g, part)).wait_recv()

    def advance(self, k):
        for f, a in self.stops(0):
            if a == k:
                if a:
                    self.arrive(0, f, 0)
                self.spread(0, f, 0)
                self.spread(1, f, 0)
        for f, a in self.stops(0):
            for g, b in self.stops(1):
                if b and a + b == k:
                    self.arrive(1, f, g)
                    self.spread(1, f, g)

    def finish(self):
        for made in self.sent:
            made.wait_send()
        self.sent = []


class Scatter:
    def __init__(self, place, terms, kind, widths, first_buf, second_buf, send_sem, recv_sem):
        self.place, self.terms, self.kind = place, terms, kind
        first = sum(widths[:kind])
        self.columns = pl.ds(first, widths[kind])
        self.bufs = (first_buf, second_buf)
        self.send_sem, self.recv_sem = send_sem, recv_sem
        self.axes = gather_axes(kind)[::-1]
        self.turns = [place.size[a] // 2 for a in self.axes]
        self.rounds = sum(self.turns)
        self.sent = {}

    def term(self, phase, at):
        axis = self.axes[phase]
        own = self.place.pos
        if phase == 1:
            x, z = (at, own["z"]) if axis == "x" else (own["x"], at)
            return self.terms.at[x, z, :, self.columns]
        if axis == "x":
            return self.terms.at[at, :, :, self.columns]
        return self.terms.at[:, at, :, self.columns]

    def slot(self, phase, d, t):
        n = self.place.size[self.axes[phase]]
        return (n // 2 if d else 0) + t - 1

    def arrived(self, phase, d, t):
        return self.bufs[phase].at[self.kind % 2, self.slot(phase, d, t)]

    def o(self, d):
        return (1 if self.kind % 2 == 0 else -1) * (1 if d == 0 else -1)

    def copy(self, phase, d, t, source):
        axis = self.axes[phase]
        first = 0 if phase == 0 else self.place.size[self.axes[0]] - 1
        return pltpu.make_async_remote_copy(
            src_ref=source,
            dst_ref=self.arrived(phase, d, t),
            send_sem=self.send_sem.at[self.kind, phase * 2 + d],
            recv_sem=self.recv_sem.at[self.kind, first + self.slot(phase, d, t)],
            device_id=self.place.neighbour(axis, self.o(d)),
            device_id_type=MESH,
        )

    def send(self, phase, d, t, source):
        before = self.sent.pop((phase, d), None)
        if before is not None:
            before.wait_send()
        made = self.copy(phase, d, t, source)
        made.start()
        self.sent[(phase, d)] = made

    def dest(self, phase, d, t, count):
        axis = self.axes[phase]
        return wrap(self.place.pos[axis] + self.o(d) * (count - t + 1), self.place.size[axis])

    def begin(self, phase):
        for d, count in ring_dirs(self.place.size[self.axes[phase]]):
            self.send(phase, d, 1, self.term(phase, self.dest(phase, d, 1, count)))

    def advance(self, k):
        if k == 0:
            self.begin(0)
            return
        phase = 0 if k <= self.turns[0] else 1
        t = k - (self.turns[0] if phase else 0)
        axis = self.axes[phase]
        dirs = ring_dirs(self.place.size[axis])
        for d, count in dirs:
            if t <= count:
                held = self.arrived(phase, d, t)
                self.copy(phase, d, t, held).wait_recv()
                if t < count:
                    held[...] = held[...] + self.term(phase, self.dest(phase, d, t + 1, count))[...]
                    self.send(phase, d, t + 1, held)
        if t == self.turns[phase]:
            own = self.term(phase, self.place.pos[axis])
            total = own[...].astype(F32)
            for d, count in dirs:
                total = total + self.arrived(phase, d, count)[...].astype(F32)
            if phase == 0:
                own[...] = total.astype(BF16)
                self.begin(1)
            else:
                self.result = total

    def finish(self):
        for made in self.sent.values():
            made.wait_send()
        self.sent = {}


class DirectGather:
    def __init__(self, place, buf, sems):
        self.place, self.buf, self.sems = place, buf, sems

    def copies(self, phase, sending):
        place = self.place
        axis = "xz"[phase]
        n = place.size[axis]
        made = []
        for j in range(1, n):
            if phase == 0:
                at = place.pos["x"] if sending else wrap(place.pos["x"] - j, n)
                ref = self.buf.at[at, place.pos["z"]]
            else:
                at = place.pos["z"] if sending else wrap(place.pos["z"] - j, n)
                ref = self.buf.at[:, at]
            made.append(
                pltpu.make_async_remote_copy(
                    src_ref=ref,
                    dst_ref=ref,
                    send_sem=self.sems.at[0, phase, j],
                    recv_sem=self.sems.at[1, phase, j],
                    device_id=place.neighbour(axis, j),
                    device_id_type=MESH,
                )
            )
        return made

    def begin(self, phase):
        for made in self.copies(phase, True):
            made.start()

    def wait(self, phase):
        for made in self.copies(phase, False):
            made.wait_recv()

    def finish(self):
        for phase in range(2):
            for made in self.copies(phase, True):
                made.wait_send()


class DirectScatter:
    def __init__(self, place, terms, first_buf, second_buf, sems):
        self.place, self.terms, self.sems = place, terms, sems
        self.bufs = (first_buf, second_buf)

    def term(self, phase, at):
        if phase == 0:
            return self.terms.at[:, at]
        return self.terms.at[at, self.place.pos["z"]]

    def copies(self, phase):
        place = self.place
        axis = "zx"[phase]
        n = place.size[axis]
        return [
            pltpu.make_async_remote_copy(
                src_ref=self.term(phase, wrap(place.pos[axis] + j, n)),
                dst_ref=self.bufs[phase].at[j],
                send_sem=self.sems.at[0, phase, j],
                recv_sem=self.sems.at[1, phase, j],
                device_id=place.neighbour(axis, j),
                device_id_type=MESH,
            )
            for j in range(1, n)
        ]

    def begin(self, phase):
        for made in self.copies(phase):
            made.start()

    def wait(self, phase):
        axis = "zx"[phase]
        for made in self.copies(phase):
            made.wait_recv()
        own = self.term(phase, self.place.pos[axis])
        total = own[...].astype(F32)
        for j in range(1, self.place.size[axis]):
            total = total + self.bufs[phase][j].astype(F32)
        if phase == 0:
            own[...] = total.astype(BF16)
        else:
            self.result = total

    def finish(self):
        for phase in range(2):
            for made in self.copies(phase):
                made.wait_send()


class RankSum:
    def __init__(self, place, parts, arrived, whole, sems):
        self.place, self.parts, self.got, self.whole, self.sems = place, parts, arrived, whole, sems

    def scatter_copy(self, j):
        peer = self.place.peer(j)
        return pltpu.make_async_remote_copy(
            src_ref=self.parts.at[peer[1]],
            dst_ref=self.got.at[j],
            send_sem=self.sems.at[0, j],
            recv_sem=self.sems.at[1, j],
            device_id=peer,
            device_id_type=MESH,
        )

    def gather_copy(self, j, at):
        return pltpu.make_async_remote_copy(
            src_ref=self.whole.at[at],
            dst_ref=self.whole.at[at],
            send_sem=self.sems.at[2, j],
            recv_sem=self.sems.at[3, j],
            device_id=self.place.peer(j),
            device_id_type=MESH,
        )

    def each(self, body):
        @pl.loop(1, self.place.nh)
        def _(j):
            body(j)

    def start(self):
        self.each(lambda j: self.scatter_copy(j).start())

    def middle(self):
        self.each(lambda j: self.scatter_copy(j).wait_recv())
        me = self.place.hid
        total = self.parts[me].astype(F32)
        for j in range(1, self.place.nh):
            total = total + self.got[j].astype(F32)
        self.whole[me] = total.astype(BF16)
        self.each(lambda j: self.gather_copy(j, me).start())

    def end(self):
        nh = self.place.nh

        def wait(j):
            self.gather_copy(j, lax.rem(self.place.hid + nh - j, nh)).wait_recv()

        self.each(wait)

    def finish(self):
        def wait(j):
            self.scatter_copy(j).wait_send()
            self.gather_copy(j, self.place.hid).wait_send()

        self.each(wait)


def layer(
    nx, nz, nh, scale,
    x_ref, g_ref, home, bu_ref, bd_ref, ul_ref, ur_ref, dl_ref, dr_ref,
    out_ref, ig_ref, gbu_ref, gbd_ref, gul_ref, gur_ref, gdl_ref, gdr_ref,
    g_low, g_all, t_low, t_all,
    low_first, low_second, all_z1, all_x2, all_x1, all_z2,
    w_up, w_down, m_one, m_two, xs, gs, xt, own_sum, hid_t, gp, hid_m, gp_m,
    rank_parts, rank_got, rank_one, rank_two,
    side_send, side_mid, side_end,
    ag_send, ag_recv, rs_send, rs_recv, rank_sems, low_sems, y_sems,
):
    place = Place(nx, nz, nh)
    rows, blk = bu_ref.shape[2], bu_ref.shape[3]
    tokens = x_ref.shape[0]
    hb = bu_ref.shape[0]
    half = rows // 2
    px, pz = place.pos["x"], place.pos["z"]

    barrier = pltpu.get_barrier_semaphore()
    for axis in ("x", "z"):
        for o in range(1, place.size[axis]):
            pl.semaphore_signal(barrier, inc=1, device_id=place.neighbour(axis, o), device_id_type=MESH)

    @pl.loop(1, nh)
    def _(j):
        pl.semaphore_signal(barrier, inc=1, device_id=place.peer(j), device_id_type=MESH)

    hidden_dev, width_dev = ur_ref.shape[1], dr_ref.shape[1]
    g_low[px, pz] = jnp.concatenate([ul_ref[...].astype(F32), dr_ref[...].astype(F32)], axis=0).astype(BF16)
    downs = SLOTS * hb * blk
    ranks = 2 * downs
    g_all[px, pz, :, ranks:] = jnp.concatenate(
        [ur_ref[...].astype(F32), dl_ref[...].astype(F32)], axis=0
    ).astype(BF16)
    for s in range(SLOTS):
        for h in range(hb):
            at = (s * hb + h) * blk
            g_all[px, pz, :, at : at + blk] = bu_ref[h, s]
            g_all[px, pz, :, downs + at : downs + at + blk] = bd_ref[h, s]
    for b in range(2):
        xs[0, b] = x_ref[:, b * blk : (b + 1) * blk]
        gs[0, b] = g_ref[:, b * blk : (b + 1) * blk]
    pl.semaphore_wait(barrier, nx + nz + nh - 3)

    gathers = [TorusGather(place, g_all, kind, ag_send, ag_recv) for kind in range(2)]
    low_gather = DirectGather(place, g_low, low_sems.at[0])
    rounds = nx // 2 + nz // 2

    def gather_step(k):
        for one_half in gathers:
            one_half.advance(k)

    part = tokens // 2
    pieces = [(ref, b, q) for ref in (xs, gs) for b in range(2) for q in range(2)]

    def y_copy(i, stage):
        ref, b, q = pieces[i]
        at = pl.ds(q * part, part)
        return pltpu.make_async_remote_copy(
            src_ref=ref.at[0 if stage == 0 else 2, b, at],
            dst_ref=ref.at[2 if stage == 0 else 1, b, at],
            send_sem=y_sems.at[stage, 0, i],
            recv_sem=y_sems.at[stage, 1, i],
            device_id=place.near if stage == 0 else place.far,
            device_id_type=MESH,
        )

    def pass_on(i):
        y_copy(i, 0).wait_recv()
        y_copy(i, 1).start()

    column = lax.broadcasted_iota(jnp.int32, (tokens, blk), 1)
    is_low = lax.rem(column, rows) < half

    def flat(buf, at, width):
        return buf[:, :, :, at : at + width].astype(F32).reshape(blk, width).astype(BF16)

    one = RankSum(place, rank_parts.at[0], rank_got.at[0], rank_one, rank_sems.at[0])
    two = RankSum(place, rank_parts.at[1], rank_got.at[1], rank_two, rank_sems.at[1])

    def rank_start(which, index, low, high):
        mixed = jnp.where(is_low, low, high).reshape(nh, tokens // nh, blk)
        rank_parts[index] = mixed.astype(BF16)
        which.start()

    def exchange(begun, passed):
        for i in begun:
            y_copy(i, 0).start()
        for i in passed:
            pass_on(i)

    low_gather.begin(0)
    gather_step(0)
    exchange((0, 1), ())
    low_gather.wait(0)
    low_gather.begin(1)
    gather_step(1)
    exchange((2, 3), (0,))
    gather_step(2)
    exchange((4, 5), (1, 2))
    low_gather.wait(1)
    for j in range(2):
        m_two[:, j * blk : (j + 1) * blk] = flat(g_low, j * blk, blk)
    rank_start(one, 0, dot(x_ref[...], m_two[...], NT), dot(g_ref[...], m_two[...], NT))
    gather_step(3)
    exchange((6, 7), (3, 4))
    gather_step(4)
    exchange((), (5, 6))
    one.middle()
    gather_step(5)
    exchange((), (7,))
    for i in range(4):
        y_copy(i, 1).wait_recv()
    for s in range(SLOTS):
        for b in range(2):
            xt[s, b] = xs[s, b].T
    for k in range(6, rounds + 1):
        gather_step(k)
    for j in range(SLOTS * hb):
        w_up[j // hb, :, (j % hb) * blk : (j % hb + 1) * blk] = flat(g_all, j * blk, blk)
        w_down[j // hb, (j % hb) * blk : (j % hb + 1) * blk, :] = flat(g_all, downs + j * blk, blk)
    for j in range(hb):
        m_one[:, j * blk : (j + 1) * blk] = flat(g_all, ranks + j * blk, blk)
    for i in range(4, 8):
        y_copy(i, 1).wait_recv()
    one.end()

    rank1 = rank_one[...].reshape(tokens, blk)
    zero = jnp.zeros_like(rank1)
    rank_in = jnp.where(is_low, rank1, zero)
    rank_back = jnp.where(is_low, zero, rank1)

    @pl.loop(0, hb)
    def _(h):
        home_h = home[h]
        at = pl.ds(pl.multiple_of(h * blk, blk), blk)
        value = dot(rank_in, m_one[:, at])
        grad = dot(rank_back, m_one[:, at])
        for s in range(SLOTS):
            value = value + dot(xs[s, home_h], w_up[s, :, at])
            grad = grad + dot(gs[s, home_h], w_down[s, at, :], NT)
        activated, derivative = gelu_pair(value)
        hidden = activated.astype(BF16)
        grad_pre = (grad * derivative).astype(BF16)
        hid_t[h] = hidden.T
        gp[h] = grad_pre
        for b in range(2):
            keep = jnp.where(home_h == b, 1.0, 0.0).astype(F32)
            hid_m[b, :, at] = (hidden.astype(F32) * keep).astype(BF16)
            gp_m[b, :, at] = (grad_pre.astype(F32) * keep).astype(BF16)

    def side(tensor, s, b):
        if tensor == 0:
            return dot(hid_m[b], w_down[s])
        return dot(gp_m[b], w_up[s], NT)

    sides = [(tensor, b) for tensor in range(2) for b in range(2)]

    def side_copy(i, stage):
        tensor, b = sides[i]
        return pltpu.make_async_remote_copy(
            src_ref=(side_send if stage == 0 else side_mid).at[tensor, b],
            dst_ref=(side_mid if stage == 0 else side_end).at[tensor, b],
            send_sem=y_sems.at[2 + stage, 0, i],
            recv_sem=y_sems.at[2 + stage, 1, i],
            device_id=place.far if stage == 0 else place.near,
            device_id_type=MESH,
        )

    hidden_all = hid_m[0] + hid_m[1]
    grad_all = gp_m[0] + gp_m[1]
    rank_start(
        two, 1, dot(grad_all, m_one[...], NT), dot(hidden_all, m_one[...], NT)
    )

    def side_begin(i):
        tensor, b = sides[i]
        side_send[tensor, b] = side(tensor, 1, b).astype(BF16)
        side_copy(i, 0).start()

    for i in range(2):
        side_begin(i)

    scatters = [
        Scatter(
            place, t_all, kind, scatter_widths(t_all.shape[3]),
            *((all_z1, all_x2) if kind < 2 else (all_x1, all_z2)),
            rs_send, rs_recv,
        )
        for kind in range(4)
    ]
    low_scatter = DirectScatter(place, t_low, low_first, low_second, low_sems.at[1])

    def scatter_step(k):
        for one_chunk in scatters:
            one_chunk.advance(k)

    def shaped(value):
        return (value * scale).reshape(nx, nz, rows, value.shape[1]).astype(BF16)

    @pl.loop(0, hb)
    def _(h):
        home_h = home[h]
        for s in range(SLOTS):
            at = pl.ds(pl.multiple_of((s * hb + h) * blk, blk), blk)
            t_all[:, :, :, at] = shaped(dot(xt[s, home_h], gp[h]))
            at = pl.ds(pl.multiple_of(downs + (s * hb + h) * blk, blk), blk)
            t_all[:, :, :, at] = shaped(dot(hid_t[h], gs[s, home_h]))

    rank_in_t = rank_in.T
    rank_back_t = rank_back.T
    for j in range(hb):
        at = slice(j * blk, (j + 1) * blk)
        t_all[:, :, :, ranks + j * blk : ranks + (j + 1) * blk] = shaped(
            dot(rank_in_t, grad_all[:, at]) + dot(rank_back_t, hidden_all[:, at])
        )
    scatter_step(0)

    def side_pass(i):
        tensor, b = sides[i]
        own = side(tensor, 2, b)
        side_copy(i, 0).wait_recv()
        side_mid[tensor, b] = (side_mid[tensor, b].astype(F32) + own).astype(BF16)
        side_copy(i, 1).start()

    scatter_step(1)
    side_begin(2)
    side_pass(0)
    two.middle()
    scatter_step(2)
    side_begin(3)
    side_pass(1)
    scatter_step(3)
    two.end()
    rank2 = rank_two[...].reshape(tokens, blk)
    rank_grad = jnp.where(is_low, rank2, zero)
    rank_mid = jnp.where(is_low, zero, rank2)
    rank_grad_t = rank_grad.T
    rank_mid_t = rank_mid.T
    for j in range(2):
        at = slice(j * blk, (j + 1) * blk)
        t_low[:, :, :, at] = shaped(dot(rank_grad_t, x_ref[:, at]) + dot(rank_mid_t, g_ref[:, at]))
    low_scatter.begin(0)

    def own_part(i):
        tensor, b = sides[i]
        at = slice(b * blk, (b + 1) * blk)
        rank = rank_mid if tensor == 0 else rank_grad
        own_sum[i] = side(tensor, 0, b) + dot(rank, m_two[:, at])

    def result(i):
        tensor, b = sides[i]
        at = slice(b * blk, (b + 1) * blk)
        total = own_sum[i]
        side_copy(i, 1).wait_recv()
        total = total + side_end[tensor, b].astype(F32)
        ref = out_ref if tensor == 0 else ig_ref
        ref[:, at] = total.astype(BF16)

    side_pass(2)
    scatter_step(4)
    side_pass(3)
    low_scatter.wait(0)
    low_scatter.begin(1)
    for i in range(4):
        own_part(i)
    result(0)
    result(1)
    scatter_step(5)
    result(2)
    for k in range(6, rounds + 1):
        scatter_step(k)
    low_scatter.wait(1)
    low = low_scatter.result
    gul_ref[...] = low[:half].astype(BF16)
    gdr_ref[...] = low[half:].astype(BF16)
    result(3)

    total = jnp.concatenate([one_chunk.result for one_chunk in scatters], axis=1)
    for first, ref in ((0, gbu_ref), (downs, gbd_ref)):
        for s in range(SLOTS):
            for h in range(hb):
                at = first + (s * hb + h) * blk
                ref[h, s] = total[:, at : at + blk].astype(BF16)
    gur_ref[...] = total[:half, ranks:].astype(BF16)
    gdl_ref[...] = total[half:, ranks:].astype(BF16)

    for one_chunk in gathers + scatters + [low_gather, low_scatter]:
        one_chunk.finish()
    for i in range(8):
        y_copy(i, 0).wait_send()
        y_copy(i, 1).wait_send()
    for i in range(4):
        side_copy(i, 0).wait_send()
        side_copy(i, 1).wait_send()
    one.finish()
    two.finish()


def hand_over(*refs):
    n = len(refs) // 2
    for source, target in zip(refs[:n], refs[n:]):
        target[...] = source[...]


def per_device(
    nx, nz, nh,
    inputs, out_grad, home_block, blocks_up, blocks_down, up_left, up_right, down_left, down_right,
):
    tokens, width_dev = inputs.shape
    hb, slots, rows, blk = blocks_up.shape
    hidden_dev = hb * blk
    scale = float(nx * nz * tokens) ** (-0.5)
    all_cols = 2 * slots * hb * blk + hidden_dev
    vmem = pl.BlockSpec(memory_space=pltpu.VMEM)
    smem = pl.BlockSpec(memory_space=pltpu.SMEM)

    def buf(shape, dtype=BF16):
        return pltpu.VMEM(shape, dtype)

    gathered = [buf((nx, nz, rows, c)) for c in (width_dev, all_cols)]
    w_z, w_x = scatter_widths(all_cols)[0], scatter_widths(all_cols)[3]
    landing = [
        buf((nz, nx, rows, width_dev)),
        buf((nx, rows, width_dev)),
        buf((2, nz - 1, nx, rows, w_z)),
        buf((2, nx - 1, rows, w_z)),
        buf((2, nx - 1, nz, rows, w_x)),
        buf((2, nz - 1, rows, w_x)),
    ]
    ups = up_left.T, down_left.T
    outs = pl.pallas_call(
        functools.partial(layer, nx, nz, nh, scale),
        out_shape=[
            jax.ShapeDtypeStruct(a.shape, BF16)
            for a in (
                inputs, out_grad, blocks_up, blocks_down, ups[0], up_right, ups[1], down_right,
            )
        ],
        in_specs=[vmem, vmem, smem] + [vmem] * 6,
        out_specs=[vmem] * 8,
        scratch_shapes=gathered
        + gathered
        + landing
        + [
            buf((slots, blk, hidden_dev)),
            buf((slots, hidden_dev, blk)),
            buf((blk, hidden_dev)),
            buf((blk, width_dev)),
            buf((slots, 2, tokens, blk)),
            buf((slots, 2, tokens, blk)),
            buf((slots, 2, blk, tokens)),
            buf((4, tokens, blk), F32),
            buf((hb, blk, tokens)),
            buf((hb, tokens, blk)),
            buf((2, tokens, hidden_dev)),
            buf((2, tokens, hidden_dev)),
            buf((2, nh, tokens // nh, blk)),
            buf((2, nh, tokens // nh, blk)),
            buf((nh, tokens // nh, blk)),
            buf((nh, tokens // nh, blk)),
            buf((2, 2, tokens, blk)),
            buf((2, 2, tokens, blk)),
            buf((2, 2, tokens, blk)),
            pltpu.SemaphoreType.DMA((2, max(nx, nz) * (min(nx, nz) + 1))),
            pltpu.SemaphoreType.DMA((2, max(nx, nz) * (min(nx, nz) + 1))),
            pltpu.SemaphoreType.DMA((4, 4)),
            pltpu.SemaphoreType.DMA((4, nx + nz - 2)),
            pltpu.SemaphoreType.DMA((2, 4, nh)),
            pltpu.SemaphoreType.DMA((2, 2, 2, max(nx, nz))),
            pltpu.SemaphoreType.DMA((4, 2, 8)),
        ],
        compiler_params=pltpu.CompilerParams(
            collective_id=0, has_side_effects=True, vmem_limit_bytes=60 * 2**20
        ),
    )(
        inputs, out_grad, home_block, blocks_up, blocks_down, ups[0], up_right, ups[1], down_right,
    )
    out, ig, gbu, gbd, gul, gur, gdl, gdr = pl.pallas_call(
        hand_over,
        out_shape=[jax.ShapeDtypeStruct(a.shape, a.dtype) for a in outs],
        in_specs=[vmem] * len(outs),
        out_specs=[vmem] * len(outs),
    )(*outs)
    return out, ig, gbu, gbd, gul.T, gur, gdl.T, gdr


def solution(mesh, nx=4):
    n_dp, nh = mesh.shape["dp"], mesh.shape["hid"]
    placed = (
        P("dp", "hid"),
        P("dp", "hid"),
        P("hid"),
        P("hid", None, "dp", None),
        P("hid", None, "dp", None),
        P("hid", "dp"),
        P("dp", "hid"),
        P("hid", "dp"),
        P("dp", "hid"),
    )
    return jax.shard_map(
        functools.partial(per_device, nx, n_dp // nx, nh),
        mesh=mesh,
        in_specs=placed,
        out_specs=(
            P("dp", "hid"),
            P("dp", "hid"),
            P("hid", None, "dp", None),
            P("hid", None, "dp", None),
            P("hid", "dp"),
            P("dp", "hid"),
            P("hid", "dp"),
            P("dp", "hid"),
        ),
        check_vma=False,
    )
```
